512 devices in a mesh: dp: 16 (over y, core), vocab: 32 (over z, x).
Axes of the slice: x: 4, y: 8, z: 8, core: 2. Of those that a mesh axis runs over, the one named last changes fastest.
Arguments:
- grad: bfloat16 [16, 4096, 3584], P('dp', 'vocab'), may hold values from -6 to 6
- error: float32 [16, 4096, 3584], P('dp', 'vocab'), may hold values from -4 to 4
- q_prev: float32 [3584, 32], replicated, may hold values from -0.09375 to 0.09375
Outputs:
- new_error: float32 [16, 4096, 3584], P('dp', 'vocab')
- p_basis: float32 [4096, 32], P('vocab')
- q_new: float32 [3584, 32], replicated
The draws below stay inside these ranges and needn't reach their ends.
All inputs are finite; a program needn't handle non-finite values.
Results may differ from the reference program's by a relative error of at most 0.0003.
Values sent between devices are 32-bit elements; how exact they have to be, the bound alone decides.
No kernel may reach another device: no remote copies, remote signals or barrier semaphores. Data moves between devices by JAX's collectives and lax.ppermute only.
A program may use at most 64 MiB of HBM per device.

```python
import jax
import jax.numpy as jnp
from jax import lax

D = 3584
RANK = 32
REPLICAS = 16
VROWS = 4096


def block_levels(key, dims, shards, least, largest):
    factor_of, own = 1.0, jax.random.fold_in(key, 6)
    for axis_at, parts in shards:
        draws = jnp.exp(jax.random.uniform(jax.random.fold_in(own, axis_at), (parts,), jnp.float32, least / len(shards), largest / len(shards)))
        factor_of = factor_of * jnp.repeat(draws, dims[axis_at] // parts).reshape([-1 if axis == axis_at else 1 for axis in range(len(dims))])
    return factor_of


def scatter_about(own_key, shape, spread, bound, cuts=(), kind=jnp.bfloat16):
    level = block_levels(own_key, shape, cuts, -0.22, 0.18) if cuts else 1.0
    array = jax.random.normal(own_key, shape, jnp.float32) * spread * level
    return jnp.minimum(jnp.maximum(array, -bound), bound).astype(kind)


def setup_inputs(seed: int = 0) -> dict:
    key_of = jax.random.split(jax.random.key(seed), 4)
    return {
        "grad": scatter_about(key_of[0], (REPLICAS, VROWS, D), 1.0, 6.0, ((0, 16), (1, 32))),
        "error": scatter_about(key_of[1], (REPLICAS, VROWS, D), 0.5, 4.0, ((0, 16), (1, 32)), jnp.float32),
        "q_prev": scatter_about(key_of[2], (D, RANK), D ** -0.5, 0.09375, (), jnp.float32),
    }


def reference(grad, error, q_prev):
    highest = lax.Precision.HIGHEST
    merged = grad.astype(jnp.float32) + error
    p_sum = jnp.einsum('rvd,dk->vk', merged, q_prev, precision=highest)
    gram = jnp.dot(p_sum.T, p_sum, precision=highest)
    chol = jnp.linalg.cholesky(gram)
    p_basis = lax.linalg.triangular_solve(chol, p_sum, left_side=False, lower=True, transpose_a=True)
    q_new = jnp.einsum('rvd,vk->dk', merged, p_basis, precision=highest) / REPLICAS
    approx = jnp.dot(p_basis, q_new.T, precision=highest)
    new_error = merged - approx[None]
    return (new_error, p_basis, q_new)
```

```python
import jax
import jax.numpy as jnp
from jax import lax
from jax.sharding import Mesh, PartitionSpec as P

HIGHEST = lax.Precision.HIGHEST
HIGH = lax.Precision.HIGH
DP = ("y", "core")
VOCAB = ("z", "x")


def gather_by_exchange(value, axes):
    members = lax.axis_size(axes)
    return lax.all_to_all(jnp.broadcast_to(value[None], (members,) + value.shape), axes, 0, 0)


def sum_by_exchange(value, axes):
    return jnp.sum(gather_by_exchange(value, axes), axis=0)


def per_device(grad, error, q_prev):
    rows, width = grad.shape[1:]
    rank = q_prev.shape[1]
    replicas = lax.axis_size(DP)
    half = width // 2
    core = lax.axis_index("core")
    merged = grad[0].astype(jnp.float32) + error[0]

    given = lax.dynamic_slice_in_dim(merged, (1 - core) * half, half, axis=1)
    taken = lax.ppermute(given, "core", [(0, 1), (1, 0)])

    p_local = lax.dot_general(q_prev, merged, (((0,), (1,)), ((), ())), precision=HIGHEST)
    p_sum = sum_by_exchange(p_local, DP)
    gram = lax.dot_general(p_sum, p_sum, (((1,), (1,)), ((), ())), precision=HIGHEST)

    chip_half = lax.dynamic_slice_in_dim(merged, core * half, half, axis=1) + taken
    right = jnp.dot(p_sum, chip_half, precision=HIGHEST)

    ny = lax.axis_size("y")
    pieces = right.reshape(rank // 8, 8, 2, half // 2).transpose(0, 2, 1, 3).reshape(ny, 8, half // 2)
    piece = jnp.sum(lax.all_to_all(pieces, "y", 0, 0), axis=0)

    packed_gram = gram.reshape(4, 8, rank).transpose(1, 0, 2).reshape(8, 4 * rank)
    packed = jnp.concatenate([piece, packed_gram], axis=1)
    packed = sum_by_exchange(packed, "x")
    packed = sum_by_exchange(packed, "z")
    piece, packed_gram = packed[:, : half // 2], packed[:, half // 2 :]
    gram = packed_gram.reshape(8, 4, rank).transpose(1, 0, 2).reshape(rank, rank)

    chol = jnp.linalg.cholesky(gram)
    inverse = lax.linalg.triangular_solve(chol, jnp.eye(rank, dtype=jnp.float32), left_side=True, lower=True)
    basis = jnp.dot(inverse, p_sum, precision=HIGHEST)

    own_half = gather_by_exchange(piece, "y")
    whole = lax.all_gather(own_half, "core")
    right = whole.reshape(2, rank // 8, 2, 8, half // 2).transpose(1, 3, 0, 2, 4).reshape(rank, width)
    q_new = jnp.dot(inverse / replicas, right, precision=HIGHEST)
    approx = lax.dot_general(basis, q_new, (((0,), (0,)), ((), ())), precision=HIGH)
    new_error = merged - approx
    return (new_error[None], basis.T, q_new.T)


def solution(mesh):
    fine = Mesh(mesh.devices.reshape(8, 2, 8, 4), DP + VOCAB)
    placed = (P(DP, VOCAB, None), P(DP, VOCAB, None), P())
    return jax.shard_map(
        per_device,
        mesh=fine,
        in_specs=placed,
        out_specs=(P(DP, VOCAB, None), P(VOCAB, None), P()),
        check_vma=False,
    )
```

```python
import functools

import jax
import jax.numpy as jnp
from jax import lax
from jax.experimental import pallas as pl
from jax.experimental.pallas import tpu as pltpu
from jax.sharding import Mesh, PartitionSpec as P

F32, BF16 = jnp.float32, jnp.bfloat16
HIGHEST = lax.Precision.HIGHEST
DP = ("y", "core")
VOCAB = ("z", "x")
NY, NX, NZ = 8, 4, 8
RANK, ROWS, WIDTH = 32, 128, 3584
HALF = WIDTH // 2
LANES = 128
TILES = HALF // LANES
PIECE = TILES + 2
VMEM_LIMIT = 48 * 1024 * 1024

NT = (((1,), (1,)), ((), ()))
NN = (((1,), (0,)), ((), ()))


def split3(value):
    high = value.astype(BF16)
    rest = value - high.astype(F32)
    middle = rest.astype(BF16)
    low = (rest - middle.astype(F32)).astype(BF16)
    return high, middle, low


def dot(a, b, dims=NN):
    return lax.dot_general(a, b, dims, preferred_element_type=F32)


def stack_left(value):
    h, m, l = split3(value)
    return jnp.concatenate([h, h, m, m, h, l], axis=1)


def stack_right(value):
    h, m, l = split3(value)
    return jnp.concatenate([h, m, h, m, l, h], axis=0)


def kernel_call(body, out_shape, **options):
    return pl.pallas_call(
        body,
        out_shape=out_shape,
        compiler_params=pltpu.CompilerParams(vmem_limit_bytes=VMEM_LIMIT),
        **options,
    )


def shape(*dims):
    return jax.ShapeDtypeStruct(dims, F32)


def left_body(core_ref, grad_ref, error_ref, q_ref, p_ref, given_ref):
    step = pl.program_id(0)
    merged = grad_ref[...].astype(F32) + error_ref[...]

    @pl.when(step == 0)
    def _():
        given_ref[...] = merged

    left = jnp.concatenate(split3(merged), axis=0)
    right = jnp.concatenate(split3(q_ref[...]), axis=0)
    product = dot(left, right, NT)
    total = product[:ROWS]
    for part in range(1, 3):
        total += product[part * ROWS : (part + 1) * ROWS]
    total = total[:, :RANK] + (total[:, RANK : 2 * RANK] + total[:, 2 * RANK :])

    @pl.when(step == 0)
    def _():
        p_ref[...] = total.T

    @pl.when(step == 1)
    def _():
        p_ref[...] += total.T


def left_product(core, grad, error, q_rows):
    columns = lambda j, core: (0, (1 - core[0] + j) % 2)
    return pl.pallas_call(
        left_body,
        out_shape=(shape(RANK, ROWS), shape(ROWS, HALF)),
        grid_spec=pltpu.PrefetchScalarGridSpec(
            num_scalar_prefetch=1,
            grid=(2,),
            in_specs=[
                pl.BlockSpec((ROWS, HALF), columns),
                pl.BlockSpec((ROWS, HALF), columns),
                pl.BlockSpec((RANK, HALF), columns),
            ],
            out_specs=[
                pl.BlockSpec((RANK, ROWS), lambda j, core: (0, 0)),
                pl.BlockSpec((ROWS, HALF), lambda j, core: (0, 0)),
            ],
        ),
        compiler_params=pltpu.CompilerParams(vmem_limit_bytes=VMEM_LIMIT),
    )(core, grad, error, q_rows)


def right_body(place_ref, parts_ref, grad_ref, error_ref, taken_ref, pieces_ref, p_ref):
    p_sum = jnp.sum(parts_ref[...], axis=0)
    p_ref[...] = p_sum
    columns = grad_ref[...].astype(F32) + error_ref[...] + taken_ref[...]
    p_parts = jnp.concatenate(split3(p_sum), axis=0)
    h, m, l = split3(columns)
    with_h = dot(p_parts, h)
    with_m = dot(p_parts[: 2 * RANK], m)
    with_l = dot(p_parts[:RANK], l)
    small = with_h[2 * RANK :] + with_m[RANK:] + with_l
    product = with_h[:RANK] + (with_h[RANK : 2 * RANK] + with_m[:RANK] + small)
    for tile in range(TILES):
        pieces_ref[:, tile, :] = product[:, tile * LANES : (tile + 1) * LANES]
    gram = lax.dot_general(p_sum, p_sum, NT, precision=HIGHEST, preferred_element_type=F32)
    packed = jnp.concatenate([gram[8 * a : 8 * a + 8] for a in range(4)], axis=1)
    mine = lax.broadcasted_iota(jnp.int32, (8, LANES), 0) == place_ref[1]
    row = jnp.sum(jnp.where(mine, packed, 0.0), axis=0, keepdims=True)
    pieces_ref[:, TILES, :] = jnp.broadcast_to(row, (RANK, LANES))
    pieces_ref[:, TILES + 1, :] = jnp.zeros((RANK, LANES), F32)


def right_product(place, parts, grad, error, taken):
    columns = lambda j, place: (0, place[0])
    whole = lambda j, place: (0, 0)
    return pl.pallas_call(
        right_body,
        out_shape=(shape(RANK, PIECE, LANES), shape(RANK, ROWS)),
        grid_spec=pltpu.PrefetchScalarGridSpec(
            num_scalar_prefetch=1,
            grid=(1,),
            in_specs=[
                pl.BlockSpec((NY, RANK, ROWS), lambda j, place: (0, 0, 0)),
                pl.BlockSpec((ROWS, HALF), columns),
                pl.BlockSpec((ROWS, HALF), columns),
                pl.BlockSpec((ROWS, HALF), whole),
            ],
            out_specs=[
                pl.BlockSpec((RANK, PIECE, LANES), lambda j, place: (0, 0, 0)),
                pl.BlockSpec((RANK, ROWS), whole),
            ],
        ),
        compiler_params=pltpu.CompilerParams(vmem_limit_bytes=VMEM_LIMIT),
    )(place, parts, grad, error, taken)


def plane_body(parts_ref, out_ref):
    rows = parts_ref[0]
    for member in range(1, NY * NX):
        rows += parts_ref[member]
    gram = [sum(parts_ref[y * NX + x, TILES : TILES + 1, :] for x in range(NX)) for y in range(NY)]
    both = jnp.concatenate([rows] + gram, axis=0)
    for z in range(NZ):
        out_ref[z] = both


def line_body(parts_ref, out_ref):
    rows = parts_ref[0, :PIECE, :]
    for z in range(1, NZ):
        rows += parts_ref[z, :PIECE, :]
    for member in range(NY * NX):
        out_ref[member] = rows


def factor_body(replicas, parts_ref, p_ref, basis_ref, basis_stack_ref, inverse_stack_ref):
    packed = parts_ref[0, PIECE:, :]
    for z in range(1, NZ):
        packed += parts_ref[z, PIECE:, :]
    gram = jnp.concatenate([packed[:, RANK * a : RANK * (a + 1)] for a in range(4)], axis=0)
    row = lax.broadcasted_iota(jnp.int32, (RANK, RANK), 0)
    column = lax.broadcasted_iota(jnp.int32, (RANK, RANK), 1)
    unit = jnp.where(row == column, 1.0, 0.0).astype(F32)
    work = jnp.concatenate([gram, unit], axis=1)
    below = lax.broadcasted_iota(jnp.int32, (RANK, 1), 0)
    inverse = []
    for j in range(RANK):
        pivot_row = work[j : j + 1, :]
        pivot = pivot_row[:, j : j + 1]
        inverse.append(pivot_row[:, RANK:] / jnp.sqrt(pivot))
        if j < RANK - 1:
            factor = jnp.where(below > j, work[:, j : j + 1] / pivot, 0.0)
            work = work - factor * pivot_row
    inverse = jnp.concatenate(inverse, axis=0)
    basis = lax.dot_general(inverse, p_ref[...], NN, precision=HIGHEST, preferred_element_type=F32)
    basis_ref[...] = basis
    basis_stack_ref[...] = stack_left(basis.T)
    inverse_stack_ref[...] = stack_left(inverse * (1.0 / replicas))


def final_body(parts_ref, inverse_ref, basis_ref, grad_ref, error_ref, out_ref, q_ref):
    right = jnp.concatenate([parts_ref[0, :, tile, :] for tile in range(TILES)], axis=1)
    q_new = dot(inverse_ref[...], stack_right(right))
    q_ref[...] = q_new
    approx = dot(basis_ref[...], stack_right(q_new))
    out_ref[...] = (grad_ref[...].astype(F32) + error_ref[...]) - approx


def final(parts, inverse_stack, basis_stack, grad, error):
    columns = lambda j: (0, j)
    whole = lambda j: (0, 0)
    return kernel_call(
        final_body,
        (shape(ROWS, WIDTH), shape(RANK, WIDTH)),
        grid=(2,),
        in_specs=[
            pl.BlockSpec((1, RANK, PIECE, LANES), lambda j: (j, 0, 0, 0)),
            pl.BlockSpec((RANK, 6 * RANK), whole),
            pl.BlockSpec((ROWS, 6 * RANK), whole),
            pl.BlockSpec((ROWS, HALF), columns),
            pl.BlockSpec((ROWS, HALF), columns),
        ],
        out_specs=[pl.BlockSpec((ROWS, HALF), columns), pl.BlockSpec((RANK, HALF), columns)],
    )(parts, inverse_stack, basis_stack, grad, error)


def per_device(grad, error, q_prev):
    grad, error = grad[0], error[0]
    replicas = lax.axis_size(DP)
    place = jnp.stack([lax.axis_index("core"), lax.axis_index("y")]).astype(jnp.int32)

    p_local, given = left_product(place, grad, error, q_prev.T)
    taken = lax.ppermute(given, "core", [(0, 1), (1, 0)])
    p_chip = jnp.sum(lax.all_gather(p_local, "core"), axis=0)
    p_parts = lax.all_to_all(jnp.broadcast_to(p_chip[None], (NY, RANK, ROWS)), "y", 0, 0)

    pieces, p_sum = right_product(place, p_parts, grad, error, taken)
    pieces = lax.all_to_all(pieces, ("y", "x"), 0, 0)
    lines = kernel_call(plane_body, shape(NZ, PIECE + 8, LANES))(pieces)
    lines = lax.all_to_all(lines, "z", 0, 0)
    own = kernel_call(line_body, shape(NY * NX, PIECE, LANES))(lines)
    own = lax.all_to_all(own, ("y", "x"), 0, 0)
    basis, basis_stack, inverse_stack = kernel_call(
        functools.partial(factor_body, replicas),
        (
            shape(RANK, ROWS),
            jax.ShapeDtypeStruct((ROWS, 6 * RANK), BF16),
            jax.ShapeDtypeStruct((RANK, 6 * RANK), BF16),
        ),
    )(lines, p_sum)
    whole = lax.all_gather(own, "core")
    new_error, q_new = final(whole, inverse_stack, basis_stack, grad, error)
    return (new_error[None], basis.T, q_new.T)


def solution(mesh):
    fine = Mesh(mesh.devices.reshape(NY, 2, NZ, NX), DP + VOCAB)
    placed = (P(DP, VOCAB, None), P(DP, VOCAB, None), P())
    return jax.shard_map(
        per_device,
        mesh=fine,
        in_specs=placed,
        out_specs=(P(DP, VOCAB, None), P(VOCAB, None), P()),
        check_vma=False,
    )
```

```python
import functools

import jax
import jax.numpy as jnp
from jax import lax
from jax.experimental import pallas as pl
from jax.experimental.pallas import tpu as pltpu
from jax.sharding import Mesh, PartitionSpec as P

F32, BF16 = jnp.float32, jnp.bfloat16
HIGHEST = lax.Precision.HIGHEST
DP = ("y", "core")
VOCAB = ("z", "x")
NY, NX, NZ = 8, 4, 8
RANK, ROWS, WIDTH = 32, 128, 3584
HALF = WIDTH // 2
LANES = 128
TILES = HALF // LANES
PIECE = TILES + 2
VMEM_LIMIT = 48 * 1024 * 1024
LEFT_CHUNKS = (1024, 1024, 1024, 512)
ANY = pl.BlockSpec(memory_space=pl.ANY)
VMEM = pl.BlockSpec(memory_space=pltpu.VMEM)

NT = (((1,), (1,)), ((), ()))
NN = (((1,), (0,)), ((), ()))


def split3(value):
    high = value.astype(BF16)
    rest = value - high.astype(F32)
    middle = rest.astype(BF16)
    low = (rest - middle.astype(F32)).astype(BF16)
    return high, middle, low


def dot(a, b, dims=NN):
    return lax.dot_general(a, b, dims, preferred_element_type=F32)


def stack_left(value):
    h, m, l = split3(value)
    return jnp.concatenate([h, h, m, m, h, l], axis=1)


def stack_right(value):
    h, m, l = split3(value)
    return jnp.concatenate([h, m, h, m, l, h], axis=0)


def kernel_call(body, out_shape, **options):
    return pl.pallas_call(
        body,
        out_shape=out_shape,
        compiler_params=pltpu.CompilerParams(vmem_limit_bytes=VMEM_LIMIT),
        **options,
    )


def vmem_call(body, out_shape):
    def call(*operands):
        return kernel_call(body, out_shape)(
            *(pltpu.with_memory_space_constraint(value, pltpu.VMEM) for value in operands)
        )

    return call


def shape(*dims):
    return jax.ShapeDtypeStruct(dims, F32)


def in_vmem(*dims, dtype=F32):
    return pltpu.VMEM(dims, dtype)


def left_body(grad_ref, error_ref, q_ref, p_ref, merged_ref, grad_buf, error_buf, q_buf, sems):
    plan, start = [], 0
    for at, size in enumerate(LEFT_CHUNKS):
        columns = pl.ds(start, size)
        copies = [
            pltpu.make_async_copy(ref.at[:, columns], buf.at[:, columns], sems.at[which, at])
            for which, (ref, buf) in enumerate(((grad_ref, grad_buf), (error_ref, error_buf), (q_ref, q_buf)))
        ]
        for copy in copies:
            copy.start()
        plan.append((slice(start, start + size), copies))
        start += size
    total = None
    for columns, copies in plan:
        for copy in copies:
            copy.wait()
        merged = grad_buf[:, columns].astype(F32) + error_buf[:, columns]
        merged_ref[:, columns] = merged
        left = jnp.concatenate(split3(q_buf[:, columns]), axis=0)
        right = jnp.concatenate(split3(merged), axis=0)
        product = dot(left, right, NT)
        total = product if total is None else total + product
    total = total[:RANK] + (total[RANK : 2 * RANK] + total[2 * RANK :])
    p_ref[...] = total[:, :ROWS] + (total[:, ROWS : 2 * ROWS] + total[:, 2 * ROWS :])


def left_product(grad, error, q_rows):
    return kernel_call(
        left_body,
        (in_vmem(RANK, ROWS), in_vmem(ROWS, WIDTH)),
        in_specs=[ANY] * 3,
        out_specs=(VMEM, VMEM),
        scratch_shapes=[
            pltpu.VMEM((ROWS, WIDTH), BF16),
            pltpu.VMEM((ROWS, WIDTH), F32),
            pltpu.VMEM((RANK, WIDTH), F32),
            pltpu.SemaphoreType.DMA((3, len(LEFT_CHUNKS))),
        ],
    )(*(pltpu.with_memory_space_constraint(value, pltpu.HBM) for value in (grad, error, q_rows)))


def right_body(mine_ref, parts_ref, chip_ref, pieces_ref, p_ref):
    p_sum = jnp.sum(parts_ref[...], axis=0)
    p_ref[...] = p_sum
    p_parts = jnp.concatenate(split3(p_sum), axis=0)
    h, m, l = split3(chip_ref[...])
    with_h = dot(p_parts, h)
    with_m = dot(p_parts[: 2 * RANK], m)
    with_l = dot(p_parts[:RANK], l)
    small = with_h[2 * RANK :] + with_m[RANK:] + with_l
    product = with_h[:RANK] + (with_h[RANK : 2 * RANK] + with_m[:RANK] + small)
    for tile in range(TILES):
        pieces_ref[:, tile, :] = product[:, tile * LANES : (tile + 1) * LANES]
    gram = lax.dot_general(p_sum, p_sum, NT, precision=HIGHEST, preferred_element_type=F32)
    packed = jnp.concatenate([gram[8 * a : 8 * a + 8] for a in range(4)], axis=1)
    row = jnp.sum(packed * mine_ref[...], axis=0, keepdims=True)
    pieces_ref[:, TILES, :] = jnp.broadcast_to(row, (RANK, LANES))
    pieces_ref[:, TILES + 1, :] = jnp.zeros((RANK, LANES), F32)


def right_product(mine, parts, chip_half):
    return vmem_call(right_body, (in_vmem(RANK, PIECE, LANES), in_vmem(RANK, ROWS)))(mine, parts, chip_half)


def plane_body(parts_ref, out_ref):
    rows = parts_ref[0]
    for member in range(1, NY * NX):
        rows += parts_ref[member]
    gram = [sum(parts_ref[y * NX + x, TILES : TILES + 1, :] for x in range(NX)) for y in range(NY)]
    both = jnp.concatenate([rows] + gram, axis=0)
    for z in range(NZ):
        out_ref[z] = both


def line_body(parts_ref, out_ref):
    rows = parts_ref[0, :PIECE, :]
    for z in range(1, NZ):
        rows += parts_ref[z, :PIECE, :]
    for member in range(NY * NX):
        out_ref[member] = rows


def factor_body(replicas, parts_ref, p_ref, basis_ref, basis_stack_ref, inverse_stack_ref):
    packed = parts_ref[0, PIECE:, :]
    for z in range(1, NZ):
        packed += parts_ref[z, PIECE:, :]
    gram = jnp.concatenate([packed[:, RANK * a : RANK * (a + 1)] for a in range(4)], axis=0)
    row = lax.broadcasted_iota(jnp.int32, (RANK, RANK), 0)
    column = lax.broadcasted_iota(jnp.int32, (RANK, RANK), 1)
    unit = jnp.where(row == column, 1.0, 0.0).astype(F32)
    work = jnp.concatenate([gram, unit], axis=1)
    below = lax.broadcasted_iota(jnp.int32, (RANK, 1), 0)
    inverse = []
    for j in range(RANK):
        pivot_row = work[j : j + 1, :]
        pivot = pivot_row[:, j : j + 1]
        inverse.append(pivot_row[:, RANK:] / jnp.sqrt(pivot))
        if j < RANK - 1:
            factor = jnp.where(below > j, work[:, j : j + 1] / pivot, 0.0)
            work = work - factor * pivot_row
    inverse = jnp.concatenate(inverse, axis=0)
    basis = lax.dot_general(inverse, p_ref[...], NN, precision=HIGHEST, preferred_element_type=F32)
    basis_ref[...] = basis
    basis_stack_ref[...] = stack_left(basis.T)
    inverse_stack_ref[...] = stack_left(inverse * (1.0 / replicas))


def final_body(parts_ref, inverse_ref, basis_ref, merged_ref, out_ref, q_ref, out_buf, q_buf, sems):
    copies = []
    for half in range(2):
        right = jnp.concatenate([parts_ref[half, :, tile, :] for tile in range(TILES)], axis=1)
        columns = slice(half * HALF, (half + 1) * HALF)
        q_new = dot(inverse_ref[...], stack_right(right))
        q_buf[:, columns] = q_new
        out_buf[:, columns] = merged_ref[:, columns] - dot(basis_ref[...], stack_right(q_new))
        for which, (buf, ref) in enumerate(((out_buf, out_ref), (q_buf, q_ref))):
            copies.append(pltpu.make_async_copy(buf.at[:, columns], ref.at[:, columns], sems.at[which, half]))
            copies[-1].start()
    for copy in copies:
        copy.wait()


def final(*operands):
    return kernel_call(
        final_body,
        (shape(ROWS, WIDTH), shape(RANK, WIDTH)),
        in_specs=[VMEM] * 4,
        out_specs=(ANY, ANY),
        scratch_shapes=[
            pltpu.VMEM((ROWS, WIDTH), F32),
            pltpu.VMEM((RANK, WIDTH), F32),
            pltpu.SemaphoreType.DMA((2, 2)),
        ],
    )(*(pltpu.with_memory_space_constraint(value, pltpu.VMEM) for value in operands))


def per_device(grad, error, q_prev):
    replicas = lax.axis_size(DP)
    core = lax.axis_index("core")
    mine = (lax.broadcasted_iota(jnp.int32, (8, LANES), 0) == lax.axis_index("y")).astype(F32)

    p_local, merged = left_product(grad[0], error[0], q_prev.T)
    given = lax.dynamic_slice_in_dim(merged, (1 - core) * HALF, HALF, axis=1)
    own_half = lax.dynamic_slice_in_dim(merged, core * HALF, HALF, axis=1)
    p_both = lax.all_gather(p_local, "core")
    p_both, given, mine = lax.optimization_barrier((p_both, given, mine))
    taken = lax.ppermute(given, "core", [(0, 1), (1, 0)])
    p_chip = jnp.sum(p_both, axis=0)
    p_parts = lax.all_to_all(jnp.broadcast_to(p_chip[None], (NY, RANK, ROWS)), "y", 0, 0)

    pieces, p_sum = right_product(mine, p_parts, own_half + taken)
    pieces = lax.all_to_all(pieces, ("y", "x"), 0, 0)
    lines = vmem_call(plane_body, in_vmem(NZ, PIECE + 8, LANES))(pieces)
    lines = lax.all_to_all(lines, "z", 0, 0)
    own = vmem_call(line_body, in_vmem(NY * NX, PIECE, LANES))(lines)
    own = lax.all_to_all(own, ("y", "x"), 0, 0)
    basis, basis_stack, inverse_stack = vmem_call(
        functools.partial(factor_body, replicas),
        (shape(RANK, ROWS), in_vmem(ROWS, 6 * RANK, dtype=BF16), in_vmem(RANK, 6 * RANK, dtype=BF16)),
    )(lines, p_sum)
    whole = lax.all_gather(own, "core")
    new_error, q_new = final(whole, inverse_stack, basis_stack, merged)
    return (new_error[None], basis.T, q_new.T)


def solution(mesh):
    fine = Mesh(mesh.devices.reshape(NY, 2, NZ, NX), DP + VOCAB)
    placed = (P(DP, VOCAB, None), P(DP, VOCAB, None), P())
    return jax.shard_map(
        per_device,
        mesh=fine,
        in_specs=placed,
        out_specs=(P(DP, VOCAB, None), P(VOCAB, None), P()),
        check_vma=False,
    )
```

```python
import functools

import jax
import jax.numpy as jnp
from jax import lax
from jax.experimental import pallas as pl
from jax.experimental.pallas import tpu as pltpu
from jax.sharding import Mesh, PartitionSpec as P

F32, BF16 = jnp.float32, jnp.bfloat16
HIGHEST = lax.Precision.HIGHEST
NY, NX, NZ = 8, 4, 8
Y = ("y2", "y1", "y0")
Z = ("z2", "z1", "z0")
Y_FAR_FIRST = ("y1", "y0", "y2")
Z_FAR_FIRST = ("z1", "z0", "z2")
DP = Y + ("core",)
VOCAB = Z + ("x",)
PLANE = Y + ("x",)
RANK, ROWS, WIDTH = 32, 128, 3584
HALF = WIDTH // 2
LANES = 128
TILES = HALF // LANES
PIECE = TILES + 2
VMEM_LIMIT = 48 * 1024 * 1024
LEFT_CHUNKS = (1024, 1024, 1024, 512)
ANY = pl.BlockSpec(memory_space=pl.ANY)
VMEM = pl.BlockSpec(memory_space=pltpu.VMEM)

NT = (((1,), (1,)), ((), ()))
NN = (((1,), (0,)), ((), ()))


def split3(value):
    high = value.astype(BF16)
    rest = value - high.astype(F32)
    middle = rest.astype(BF16)
    low = (rest - middle.astype(F32)).astype(BF16)
    return high, middle, low


def dot(a, b, dims=NN):
    return lax.dot_general(a, b, dims, preferred_element_type=F32)


def stack_left(value):
    h, m, l = split3(value)
    return jnp.concatenate([h, h, m, m, h, l], axis=1)


def stack_right(value):
    h, m, l = split3(value)
    return jnp.concatenate([h, m, h, m, l, h], axis=0)


def kernel_call(body, out_shape, **options):
    return pl.pallas_call(
        body,
        out_shape=out_shape,
        compiler_params=pltpu.CompilerParams(vmem_limit_bytes=VMEM_LIMIT),
        **options,
    )


def vmem_call(body, out_shape):
    def call(*operands):
        return kernel_call(body, out_shape)(
            *(pltpu.with_memory_space_constraint(value, pltpu.VMEM) for value in operands)
        )

    return call


def shape(*dims):
    return jax.ShapeDtypeStruct(dims, F32)


def in_vmem(*dims, dtype=F32):
    return pltpu.VMEM(dims, dtype)


def left_body(grad_ref, error_ref, q_ref, p_ref, merged_ref, grad_buf, error_buf, q_buf, sems):
    plan, start = [], 0
    for at, size in enumerate(LEFT_CHUNKS):
        columns = pl.ds(start, size)
        copies = [
            pltpu.make_async_copy(ref.at[:, columns], buf.at[:, columns], sems.at[which, at])
            for which, (ref, buf) in enumerate(((grad_ref, grad_buf), (error_ref, error_buf), (q_ref, q_buf)))
        ]
        for copy in copies:
            copy.start()
        plan.append((slice(start, start + size), copies))
        start += size
    total = None
    for columns, copies in plan:
        for copy in copies:
            copy.wait()
        merged = grad_buf[:, columns].astype(F32) + error_buf[:, columns]
        merged_ref[:, columns] = merged
        left = jnp.concatenate(split3(q_buf[:, columns]), axis=0)
        right = jnp.concatenate(split3(merged), axis=0)
        product = dot(left, right, NT)
        total = product if total is None else total + product
    total = total[:RANK] + (total[RANK : 2 * RANK] + total[2 * RANK :])
    p_ref[...] = total[:, :ROWS] + (total[:, ROWS : 2 * ROWS] + total[:, 2 * ROWS :])


def left_product(grad, error, q_rows):
    return kernel_call(
        left_body,
        (in_vmem(RANK, ROWS), in_vmem(ROWS, WIDTH)),
        in_specs=[ANY] * 3,
        out_specs=(VMEM, VMEM),
        scratch_shapes=[
            pltpu.VMEM((ROWS, WIDTH), BF16),
            pltpu.VMEM((ROWS, WIDTH), F32),
            pltpu.VMEM((RANK, WIDTH), F32),
            pltpu.SemaphoreType.DMA((3, len(LEFT_CHUNKS))),
        ],
    )(*(pltpu.with_memory_space_constraint(value, pltpu.HBM) for value in (grad, error, q_rows)))


def right_body(mine_ref, parts_ref, merged_ref, pieces_ref, p_ref):
    p_sum = jnp.sum(parts_ref[...], axis=0)
    p_ref[...] = p_sum
    p_parts = jnp.concatenate(split3(p_sum), axis=0)
    gram = lax.dot_general(p_sum, p_sum, NT, precision=HIGHEST, preferred_element_type=F32)
    packed = jnp.concatenate([gram[8 * a : 8 * a + 8] for a in range(4)], axis=1)
    row = 0.5 * jnp.sum(packed * mine_ref[...], axis=0, keepdims=True)
    for half in range(2):
        h, m, l = split3(merged_ref[:, half * HALF : (half + 1) * HALF])
        with_h = dot(p_parts, h)
        with_m = dot(p_parts[: 2 * RANK], m)
        with_l = dot(p_parts[:RANK], l)
        small = with_h[2 * RANK :] + with_m[RANK:] + with_l
        product = with_h[:RANK] + (with_h[RANK : 2 * RANK] + with_m[:RANK] + small)
        for tile in range(TILES):
            pieces_ref[half, :, tile, :] = product[:, tile * LANES : (tile + 1) * LANES]
        pieces_ref[half, :, TILES, :] = jnp.broadcast_to(row, (RANK, LANES))
        pieces_ref[half, :, TILES + 1, :] = jnp.zeros((RANK, LANES), F32)


def right_product(mine, parts, merged):
    return vmem_call(right_body, (in_vmem(2, RANK, PIECE, LANES), in_vmem(RANK, ROWS)))(mine, parts, merged)


def plane_body(parts_ref, out_ref):
    rows = parts_ref[0]
    for member in range(1, NY * NX):
        rows += parts_ref[member]
    gram = [sum(parts_ref[y * NX + x, TILES : TILES + 1, :] for x in range(NX)) for y in range(NY)]
    both = jnp.concatenate([rows] + gram, axis=0)
    for z in range(NZ):
        out_ref[z] = both


def line_body(parts_ref, out_ref):
    rows = parts_ref[0, :PIECE, :]
    for z in range(1, NZ):
        rows += parts_ref[z, :PIECE, :]
    for member in range(NY * NX):
        out_ref[member] = rows


def factor_body(replicas, parts_ref, p_ref, basis_ref, basis_stack_ref, inverse_stack_ref):
    packed = parts_ref[0, PIECE:, :]
    for z in range(1, NZ):
        packed += parts_ref[z, PIECE:, :]
    gram = jnp.concatenate([packed[:, RANK * a : RANK * (a + 1)] for a in range(4)], axis=0)
    row = lax.broadcasted_iota(jnp.int32, (RANK, RANK), 0)
    column = lax.broadcasted_iota(jnp.int32, (RANK, RANK), 1)
    unit = jnp.where(row == column, 1.0, 0.0).astype(F32)
    work = jnp.concatenate([gram, unit], axis=1)
    below = lax.broadcasted_iota(jnp.int32, (RANK, 1), 0)
    inverse = []
    for j in range(RANK):
        pivot_row = work[j : j + 1, :]
        pivot = pivot_row[:, j : j + 1]
        inverse.append(pivot_row[:, RANK:] / jnp.sqrt(pivot))
        if j < RANK - 1:
            factor = jnp.where(below > j, work[:, j : j + 1] / pivot, 0.0)
            work = work - factor * pivot_row
    inverse = jnp.concatenate(inverse, axis=0)
    basis = lax.dot_general(inverse, p_ref[...], NN, precision=HIGHEST, preferred_element_type=F32)
    basis_ref[...] = basis
    basis_stack_ref[...] = stack_left(basis.T)
    inverse_stack_ref[...] = stack_left(inverse * (1.0 / replicas))


def final_body(parts_ref, inverse_ref, basis_ref, merged_ref, out_ref, q_ref, out_buf, q_buf, sems):
    copies = []
    for half in range(2):
        right = jnp.concatenate([parts_ref[half, :, tile, :] for tile in range(TILES)], axis=1)
        columns = slice(half * HALF, (half + 1) * HALF)
        q_new = dot(inverse_ref[...], stack_right(right))
        q_buf[:, columns] = q_new
        out_buf[:, columns] = merged_ref[:, columns] - dot(basis_ref[...], stack_right(q_new))
        for which, (buf, ref) in enumerate(((out_buf, out_ref), (q_buf, q_ref))):
            copies.append(pltpu.make_async_copy(buf.at[:, columns], ref.at[:, columns], sems.at[which, half]))
            copies[-1].start()
    for copy in copies:
        copy.wait()


def final(*operands):
    return kernel_call(
        final_body,
        (shape(ROWS, WIDTH), shape(RANK, WIDTH)),
        in_specs=[VMEM] * 4,
        out_specs=(ANY, ANY),
        scratch_shapes=[
            pltpu.VMEM((ROWS, WIDTH), F32),
            pltpu.VMEM((RANK, WIDTH), F32),
            pltpu.SemaphoreType.DMA((2, 2)),
        ],
    )(*(pltpu.with_memory_space_constraint(value, pltpu.VMEM) for value in operands))


def pick(values, at):
    return lax.dynamic_index_in_dim(values, at, keepdims=False)


def per_device(grad, error, q_prev):
    replicas = lax.axis_size(DP)
    core = lax.axis_index("core").astype(jnp.uint32)
    mine = (lax.broadcasted_iota(jnp.int32, (8, LANES), 0) == lax.axis_index(Y)).astype(F32)

    p_local, merged = left_product(grad[0], error[0], q_prev.T)
    p_both, mine, core, other = lax.optimization_barrier((lax.all_gather(p_local, "core"), mine, core, 1 - core))
    p_chip = jnp.sum(p_both, axis=0)
    p_parts = lax.all_to_all(jnp.broadcast_to(p_chip[None], (NY, RANK, ROWS)), Y_FAR_FIRST, 0, 0)

    pieces, p_sum = right_product(mine, p_parts, merged)
    traded = lax.all_gather(pick(pieces, other), "core")
    pieces = pick(pieces, core) + pick(traded, other)
    pieces = lax.all_to_all(pieces, PLANE, 0, 0)
    lines = vmem_call(plane_body, in_vmem(NZ, PIECE + 8, LANES))(pieces)
    lines = lax.all_to_all(lines, Z_FAR_FIRST, 0, 0)
    own = vmem_call(line_body, in_vmem(NY * NX, PIECE, LANES))(lines)
    own = lax.all_to_all(own, PLANE, 0, 0)
    basis, basis_stack, inverse_stack = vmem_call(
        functools.partial(factor_body, replicas),
        (shape(RANK, ROWS), in_vmem(ROWS, 6 * RANK, dtype=BF16), in_vmem(RANK, 6 * RANK, dtype=BF16)),
    )(lines, p_sum)
    whole = lax.all_gather(own, "core")
    new_error, q_new = final(whole, inverse_stack, basis_stack, merged)
    return (new_error[None], basis.T, q_new.T)


def solution(mesh):
    fine = Mesh(mesh.devices.reshape(2, 2, 2, 2, 2, 2, 2, NX), DP + VOCAB)
    placed = (P(DP, VOCAB, None), P(DP, VOCAB, None), P())
    return jax.shard_map(
        per_device,
        mesh=fine,
        in_specs=placed,
        out_specs=(P(DP, VOCAB, None), P(VOCAB, None), P()),
        check_vma=False,
    )
```

```python
import functools

import jax
import jax.numpy as jnp
from jax import lax
from jax.experimental import pallas as pl
from jax.experimental.pallas import tpu as pltpu
from jax.sharding import PartitionSpec as P

F32, BF16 = jnp.float32, jnp.bfloat16
HIGHEST = lax.Precision.HIGHEST
AXES = ("dp", "vocab")
RING, NX = 8, 4
PLANE = RING * NX


def device(y, core, z, x):
    return ((y * 2 + core) * RING + z) * NX + x


FAR_FIRST = (0, 4, 1, 5, 2, 6, 3, 7)
CHIP_GROUPS = [[device(y, c, z, x) for c in range(2)] for y in range(RING) for z in range(RING) for x in range(NX)]
Y_GROUPS = [[device(y, c, z, x) for y in FAR_FIRST] for c in range(2) for z in range(RING) for x in range(NX)]


def across(core, a, b, x):
    return device(b, core, a, x) if core else device(a, core, b, x)


PLANE_GROUPS = [
    [across(c, a, b, x) for a in range(RING) for x in range(NX)] for c in range(2) for b in range(RING)
]
LINE_GROUPS = [
    [across(c, a, b, x) for b in FAR_FIRST] for c in range(2) for a in range(RING) for x in range(NX)
]
RANK, ROWS, WIDTH = 32, 128, 3584
HALF = WIDTH // 2
LANES = 128
TILES = HALF // LANES
PIECE = TILES + 2
VMEM_LIMIT = 48 * 1024 * 1024
LEFT_CHUNKS = (1024, 1024, 1024, 512)
ANY = pl.BlockSpec(memory_space=pl.ANY)
VMEM = pl.BlockSpec(memory_space=pltpu.VMEM)

NT = (((1,), (1,)), ((), ()))
NN = (((1,), (0,)), ((), ()))


def split3(value):
    high = value.astype(BF16)
    rest = value - high.astype(F32)
    middle = rest.astype(BF16)
    low = (rest - middle.astype(F32)).astype(BF16)
    return high, middle, low


def dot(a, b, dims=NN):
    return lax.dot_general(a, b, dims, preferred_element_type=F32)


def stack_left(value):
    h, m, l = split3(value)
    return jnp.concatenate([h, h, m, m, h, l], axis=1)


def stack_right(value):
    h, m, l = split3(value)
    return jnp.concatenate([h, m, h, m, l, h], axis=0)


def kernel_call(body, out_shape, **options):
    return pl.pallas_call(
        body,
        out_shape=out_shape,
        compiler_params=pltpu.CompilerParams(vmem_limit_bytes=VMEM_LIMIT),
        **options,
    )


def vmem_call(body, out_shape):
    def call(*operands):
        return kernel_call(body, out_shape)(
            *(pltpu.with_memory_space_constraint(value, pltpu.VMEM) for value in operands)
        )

    return call


def shape(*dims):
    return jax.ShapeDtypeStruct(dims, F32)


def in_vmem(*dims, dtype=F32):
    return pltpu.VMEM(dims, dtype)


def left_body(grad_ref, error_ref, q_ref, p_ref, merged_ref, grad_buf, error_buf, q_buf, sems):
    plan, start = [], 0
    for at, size in enumerate(LEFT_CHUNKS):
        columns = pl.ds(start, size)
        copies = [
            pltpu.make_async_copy(ref.at[:, columns], buf.at[:, columns], sems.at[which, at])
            for which, (ref, buf) in enumerate(((grad_ref, grad_buf), (error_ref, error_buf), (q_ref, q_buf)))
        ]
        for copy in copies:
            copy.start()
        plan.append((slice(start, start + size), copies))
        start += size
    total = None
    for columns, copies in plan:
        for copy in copies:
            copy.wait()
        merged = grad_buf[:, columns].astype(F32) + error_buf[:, columns]
        merged_ref[:, columns] = merged
        left = jnp.concatenate(split3(q_buf[:, columns]), axis=0)
        right = jnp.concatenate(split3(merged), axis=0)
        product = dot(left, right, NT)
        total = product if total is None else total + product
    total = total[:RANK] + (total[RANK : 2 * RANK] + total[2 * RANK :])
    p_ref[...] = total[:, :ROWS] + (total[:, ROWS : 2 * ROWS] + total[:, 2 * ROWS :])


def left_product(grad, error, q_rows):
    return kernel_call(
        left_body,
        (in_vmem(RANK, ROWS), in_vmem(ROWS, WIDTH)),
        in_specs=[ANY] * 3,
        out_specs=(VMEM, VMEM),
        scratch_shapes=[
            pltpu.VMEM((ROWS, WIDTH), BF16),
            pltpu.VMEM((ROWS, WIDTH), F32),
            pltpu.VMEM((RANK, WIDTH), F32),
            pltpu.SemaphoreType.DMA((3, len(LEFT_CHUNKS))),
        ],
    )(*(pltpu.with_memory_space_constraint(value, pltpu.HBM) for value in (grad, error, q_rows)))


def right_body(place_ref, parts_ref, merged_ref, pieces_ref, p_ref):
    p_sum = jnp.sum(parts_ref[...], axis=0)
    p_ref[...] = p_sum
    p_parts = jnp.concatenate(split3(p_sum), axis=0)
    gram = lax.dot_general(p_sum, p_sum, NT, precision=HIGHEST, preferred_element_type=F32)
    packed = jnp.concatenate([gram[8 * a : 8 * a + 8] for a in range(4)], axis=1)
    row = 0.5 * jnp.sum(packed * place_ref[:8, :], axis=0, keepdims=True)
    for half in range(2):
        h, m, l = split3(merged_ref[:, half * HALF : (half + 1) * HALF])
        with_h = dot(p_parts, h)
        with_m = dot(p_parts[: 2 * RANK], m)
        with_l = dot(p_parts[:RANK], l)
        small = with_h[2 * RANK :] + with_m[RANK:] + with_l
        product = with_h[:RANK] + (with_h[RANK : 2 * RANK] + with_m[:RANK] + small)
        for tile in range(TILES):
            pieces_ref[half, :, tile, :] = product[:, tile * LANES : (tile + 1) * LANES]
        pieces_ref[half, :, TILES, :] = jnp.broadcast_to(row, (RANK, LANES))
        pieces_ref[half, :, TILES + 1, :] = jnp.zeros((RANK, LANES), F32)


def right_product(place, parts, merged):
    return vmem_call(right_body, (in_vmem(2, RANK, PIECE, LANES), in_vmem(RANK, ROWS)))(place, parts, merged)


def plane_body(place_ref, parts_ref, out_ref):
    rows = parts_ref[0]
    for member in range(1, PLANE):
        rows += parts_ref[member]
    apart = [sum(parts_ref[a * NX + x, TILES : TILES + 1, :] for x in range(NX)) for a in range(RING)]
    total = apart[FAR_FIRST[0]]
    for z in FAR_FIRST[1:]:
        total += apart[z]
    gram = jnp.where(place_ref[8:, :] > 0, total * place_ref[:8, :], jnp.concatenate(apart, axis=0))
    both = jnp.concatenate([rows, gram], axis=0)
    for member in range(RING):
        out_ref[member] = both


def line_body(parts_ref, out_ref):
    rows = parts_ref[0, :PIECE, :]
    for member in range(1, RING):
        rows += parts_ref[member, :PIECE, :]
    for member in range(PLANE):
        out_ref[member] = rows


def factor_body(replicas, parts_ref, p_ref, basis_ref, basis_stack_ref, inverse_stack_ref):
    packed = parts_ref[0, PIECE:, :]
    for member in range(1, RING):
        packed += parts_ref[member, PIECE:, :]
    gram = jnp.concatenate([packed[:, RANK * a : RANK * (a + 1)] for a in range(4)], axis=0)
    row = lax.broadcasted_iota(jnp.int32, (RANK, RANK), 0)
    column = lax.broadcasted_iota(jnp.int32, (RANK, RANK), 1)
    unit = jnp.where(row == column, 1.0, 0.0).astype(F32)
    work = jnp.concatenate([gram, unit], axis=1)
    below = lax.broadcasted_iota(jnp.int32, (RANK, 1), 0)
    inverse = []
    for j in range(RANK):
        pivot_row = work[j : j + 1, :]
        pivot = pivot_row[:, j : j + 1]
        inverse.append(pivot_row[:, RANK:] / jnp.sqrt(pivot))
        if j < RANK - 1:
            factor = jnp.where(below > j, work[:, j : j + 1] / pivot, 0.0)
            work = work - factor * pivot_row
    inverse = jnp.concatenate(inverse, axis=0)
    basis = lax.dot_general(inverse, p_ref[...], NN, precision=HIGHEST, preferred_element_type=F32)
    basis_ref[...] = basis
    basis_stack_ref[...] = stack_left(basis.T)
    inverse_stack_ref[...] = stack_left(inverse * (1.0 / replicas))


def final_body(parts_ref, inverse_ref, basis_ref, merged_ref, out_ref, q_ref, out_buf, q_buf, sems):
    copies = []
    for half in range(2):
        right = jnp.concatenate([parts_ref[half, :, tile, :] for tile in range(TILES)], axis=1)
        columns = slice(half * HALF, (half + 1) * HALF)
        q_new = dot(inverse_ref[...], stack_right(right))
        q_buf[:, columns] = q_new
        out_buf[:, columns] = merged_ref[:, columns] - dot(basis_ref[...], stack_right(q_new))
        for which, (buf, ref) in enumerate(((out_buf, out_ref), (q_buf, q_ref))):
            copies.append(pltpu.make_async_copy(buf.at[:, columns], ref.at[:, columns], sems.at[which, half]))
            copies[-1].start()
    for copy in copies:
        copy.wait()


def final(*operands):
    return kernel_call(
        final_body,
        (shape(ROWS, WIDTH), shape(RANK, WIDTH)),
        in_specs=[VMEM] * 4,
        out_specs=(ANY, ANY),
        scratch_shapes=[
            pltpu.VMEM((ROWS, WIDTH), F32),
            pltpu.VMEM((RANK, WIDTH), F32),
            pltpu.SemaphoreType.DMA((2, 2)),
        ],
    )(*(pltpu.with_memory_space_constraint(value, pltpu.VMEM) for value in operands))


def pick(values, at):
    return lax.dynamic_index_in_dim(values, at, keepdims=False)


def exchange(values, groups):
    return lax.all_to_all(values, AXES, 0, 0, axis_index_groups=groups)


def spread(value, groups):
    return exchange(jnp.broadcast_to(value[None], (len(groups[0]),) + value.shape), groups)


def both_cores(value):
    return lax.all_gather(value, AXES, axis_index_groups=CHIP_GROUPS)


def per_device(grad, error, q_prev):
    replicas = lax.axis_size("dp")
    dp = lax.axis_index("dp").astype(jnp.uint32)
    core = dp % 2
    row = lax.broadcasted_iota(jnp.uint32, (16, LANES), 0)
    place = jnp.where(row < 8, row == dp // 2, core == 1).astype(F32)

    p_local, merged = left_product(grad[0], error[0], q_prev.T)
    p_both, place, core, other = lax.optimization_barrier((both_cores(p_local), place, core, 1 - core))
    p_parts = spread(jnp.sum(p_both, axis=0), Y_GROUPS)

    pieces, p_sum = right_product(place, p_parts, merged)
    traded = both_cores(pick(pieces, other))
    pieces = exchange(pick(pieces, core) + pick(traded, other), PLANE_GROUPS)
    lines = vmem_call(plane_body, in_vmem(RING, PIECE + 8, LANES))(place, pieces)
    lines = exchange(lines, LINE_GROUPS)
    own = vmem_call(line_body, in_vmem(PLANE, PIECE, LANES))(lines)
    own = exchange(own, PLANE_GROUPS)
    basis, basis_stack, inverse_stack = vmem_call(
        functools.partial(factor_body, replicas),
        (shape(RANK, ROWS), in_vmem(ROWS, 6 * RANK, dtype=BF16), in_vmem(RANK, 6 * RANK, dtype=BF16)),
    )(lines, p_sum)
    whole = both_cores(own)
    new_error, q_new = final(whole, inverse_stack, basis_stack, merged)
    return (new_error[None], basis.T, q_new.T)


def solution(mesh):
    placed = (P("dp", "vocab", None), P("dp", "vocab", None), P())
    return jax.shard_map(
        per_device,
        mesh=mesh,
        in_specs=placed,
        out_specs=(P("dp", "vocab", None), P("vocab", None), P()),
        check_vma=False,
    )
```

```python
import functools

import jax
import jax.numpy as jnp
from jax import lax
from jax.experimental import pallas as pl
from jax.experimental.pallas import tpu as pltpu
from jax.sharding import PartitionSpec as P

F32, BF16 = jnp.float32, jnp.bfloat16
HIGHEST = lax.Precision.HIGHEST
AXES = ("dp", "vocab")
RING, NX = 8, 4
PLANE = RING * NX


def device(y, core, z, x):
    return ((y * 2 + core) * RING + z) * NX + x


FAR_FIRST = (0, 4, 1, 5, 2, 6, 3, 7)
X_ORDER = (0, 2, 1, 3)
COST = 10**10
CHIP_GROUPS = [[device(y, c, z, x) for c in range(2)] for y in range(RING) for z in range(RING) for x in range(NX)]
Y_GROUPS = [[device(y, c, z, x) for y in FAR_FIRST] for c in range(2) for z in range(RING) for x in range(NX)]


CORE_SWAP = [pair for a, b in CHIP_GROUPS for pair in ((a, b), (b, a))]


def across(core, a, b, x):
    return device(b, core, a, x) if core else device(a, core, b, x)


PLANE_GROUPS = [
    [across(c, a, b, x) for x in X_ORDER for a in range(RING)] for c in range(2) for b in range(RING)
]
LINE_GROUPS = [
    [across(c, a, b, x) for b in FAR_FIRST] for c in range(2) for a in range(RING) for x in range(NX)
]
RANK, ROWS, WIDTH = 32, 128, 3584
HALF = WIDTH // 2
QUARTER = HALF // 2
LANES = 128
TILES = HALF // LANES
PIECE = TILES + 2
VMEM_LIMIT = 48 * 1024 * 1024
LEFT_CHUNKS = (1024, 1024, 1024, 512)
ANY = pl.BlockSpec(memory_space=pl.ANY)
VMEM = pl.BlockSpec(memory_space=pltpu.VMEM)

NT = (((1,), (1,)), ((), ()))
NN = (((1,), (0,)), ((), ()))


def split3(value):
    high = value.astype(BF16)
    rest = value - high.astype(F32)
    middle = rest.astype(BF16)
    low = (rest - middle.astype(F32)).astype(BF16)
    return high, middle, low


def dot(a, b, dims=NN):
    return lax.dot_general(a, b, dims, preferred_element_type=F32)


def stack_left(value):
    h, m, l = split3(value)
    return jnp.concatenate([h, h, m, m, h, l], axis=1)


def stack_right(value):
    h, m, l = split3(value)
    return jnp.concatenate([h, m, h, m, l, h], axis=0)


def kernel_call(body, out_shape, **options):
    return pl.pallas_call(
        body,
        out_shape=out_shape,
        compiler_params=pltpu.CompilerParams(vmem_limit_bytes=VMEM_LIMIT),
        **options,
    )


def vmem_call(body, out_shape, **options):
    def call(*operands):
        return kernel_call(body, out_shape, **options)(
            *(pltpu.with_memory_space_constraint(value, pltpu.VMEM) for value in operands)
        )

    return call


def shape(*dims):
    return jax.ShapeDtypeStruct(dims, F32)


def in_vmem(*dims, dtype=F32):
    return pltpu.VMEM(dims, dtype)


def left_body(grad_ref, error_ref, q_ref, p_ref, merged_ref, grad_buf, error_buf, q_buf, sems):
    plan, start = [], 0
    for at, size in enumerate(LEFT_CHUNKS):
        columns = pl.ds(start, size)
        copies = [
            pltpu.make_async_copy(ref.at[:, columns], buf.at[:, columns], sems.at[which, at])
            for which, (ref, buf) in enumerate(((grad_ref, grad_buf), (error_ref, error_buf), (q_ref, q_buf)))
        ]
        for copy in copies:
            copy.start()
        plan.append((slice(start, start + size), copies))
        start += size
    total = None
    for columns, copies in plan:
        for copy in copies:
            copy.wait()
        merged = grad_buf[:, columns].astype(F32) + error_buf[:, columns]
        merged_ref[:, columns] = merged
        left = jnp.concatenate(split3(q_buf[:, columns]), axis=0)
        right = jnp.concatenate(split3(merged), axis=0)
        product = dot(left, right, NT)
        total = product if total is None else total + product
    total = total[:RANK] + (total[RANK : 2 * RANK] + total[2 * RANK :])
    p_ref[...] = total[:, :ROWS] + (total[:, ROWS : 2 * ROWS] + total[:, 2 * ROWS :])


def left_product(grad, error, q_rows):
    return kernel_call(
        left_body,
        (in_vmem(RANK, ROWS), in_vmem(ROWS, WIDTH)),
        in_specs=[ANY] * 3,
        out_specs=(VMEM, VMEM),
        scratch_shapes=[
            pltpu.VMEM((ROWS, WIDTH), BF16),
            pltpu.VMEM((ROWS, WIDTH), F32),
            pltpu.VMEM((RANK, WIDTH), F32),
            pltpu.SemaphoreType.DMA((3, len(LEFT_CHUNKS))),
        ],
    )(*(pltpu.with_memory_space_constraint(value, pltpu.HBM) for value in (grad, error, q_rows)))


def parts_body(place_ref, parts_ref, p_ref, split_ref, row_ref):
    p_sum = jnp.sum(parts_ref[...], axis=0)
    p_ref[...] = p_sum
    split_ref[...] = jnp.concatenate(split3(p_sum), axis=0)
    gram = lax.dot_general(p_sum, p_sum, NT, precision=HIGHEST, preferred_element_type=F32)
    packed = jnp.concatenate([gram[8 * a : 8 * a + 8] for a in range(4)], axis=1)
    row = jnp.sum(packed * place_ref[:8, :], axis=0, keepdims=True)
    row_ref[...] = jnp.broadcast_to(row, (8, LANES))


def right_body(split_ref, row_ref, own_ref, taken_ref, pieces_ref, taken_buf, sems):
    p_parts = split_ref[...]
    copies = []
    for at in range(2):
        columns = pl.ds(at * QUARTER, QUARTER)
        copies.append(pltpu.make_async_copy(taken_ref.at[:, columns], taken_buf.at[:, columns], sems.at[at]))
        copies[-1].start()
    pieces_ref[:, TILES, :] = jnp.broadcast_to(row_ref[:1, :], (RANK, LANES))
    pieces_ref[:, TILES + 1, :] = jnp.zeros((RANK, LANES), F32)
    for at in range(2):
        copies[at].wait()
        columns = slice(at * QUARTER, (at + 1) * QUARTER)
        h, m, l = split3(own_ref[:, columns] + taken_buf[:, columns])
        with_h = dot(p_parts, h)
        with_m = dot(p_parts[: 2 * RANK], m)
        with_l = dot(p_parts[:RANK], l)
        small = with_h[2 * RANK :] + with_m[RANK:] + with_l
        product = with_h[:RANK] + (with_h[RANK : 2 * RANK] + with_m[:RANK] + small)
        for tile in range(TILES // 2):
            pieces_ref[:, at * (TILES // 2) + tile, :] = product[:, tile * LANES : (tile + 1) * LANES]


def right_product(p_split, row, own_half, taken):
    local = (pltpu.with_memory_space_constraint(value, pltpu.VMEM) for value in (p_split, row, own_half))
    return kernel_call(
        right_body,
        in_vmem(RANK, PIECE, LANES),
        in_specs=[VMEM] * 3 + [ANY],
        out_specs=VMEM,
        scratch_shapes=[pltpu.VMEM((ROWS, HALF), F32), pltpu.SemaphoreType.DMA((2,))],
    )(*local, taken)


def plane_body(place_ref, parts_ref, out_ref):
    rows = parts_ref[0]
    for member in range(1, PLANE):
        rows += parts_ref[member]
    apart = [sum(parts_ref[x * RING + a, TILES : TILES + 1, :] for x in range(NX)) for a in range(RING)]
    total = apart[FAR_FIRST[0]]
    for z in FAR_FIRST[1:]:
        total += apart[z]
    gram = jnp.where(place_ref[8:, :] > 0, total * place_ref[:8, :], jnp.concatenate(apart, axis=0))
    both = jnp.concatenate([rows, gram], axis=0)
    for member in range(RING):
        out_ref[member] = both


def line_body(parts_ref, out_ref):
    rows = parts_ref[0, :PIECE, :]
    for member in range(1, RING):
        rows += parts_ref[member, :PIECE, :]
    for member in range(PLANE):
        out_ref[member] = rows


def factor_body(replicas, parts_ref, p_ref, basis_ref, basis_stack_ref, inverse_stack_ref):
    packed = parts_ref[0, PIECE:, :]
    for member in range(1, RING):
        packed += parts_ref[member, PIECE:, :]
    gram = jnp.concatenate([packed[:, RANK * a : RANK * (a + 1)] for a in range(4)], axis=0)
    row = lax.broadcasted_iota(jnp.int32, (RANK, RANK), 0)
    column = lax.broadcasted_iota(jnp.int32, (RANK, RANK), 1)
    unit = jnp.where(row == column, 1.0, 0.0).astype(F32)
    work = jnp.concatenate([gram, unit], axis=1)
    below = lax.broadcasted_iota(jnp.int32, (RANK, 1), 0)
    inverse = []
    for j in range(RANK):
        pivot_row = work[j : j + 1, :]
        pivot = pivot_row[:, j : j + 1]
        inverse.append(pivot_row[:, RANK:] / jnp.sqrt(pivot))
        if j < RANK - 1:
            factor = jnp.where(below > j, work[:, j : j + 1] / pivot, 0.0)
            work = work - factor * pivot_row
    inverse = jnp.concatenate(inverse, axis=0)
    basis = lax.dot_general(inverse, p_ref[...], NN, precision=HIGHEST, preferred_element_type=F32)
    basis_ref[...] = basis
    basis_stack_ref[...] = stack_left(basis.T)
    inverse_stack_ref[...] = stack_left(inverse * (1.0 / replicas))


def final_body(parts_ref, inverse_ref, basis_ref, merged_ref, out_ref, q_ref, out_buf, q_buf, sems):
    copies = []
    for half in range(2):
        right = jnp.concatenate([parts_ref[half, :, tile, :] for tile in range(TILES)], axis=1)
        columns = slice(half * HALF, (half + 1) * HALF)
        q_new = dot(inverse_ref[...], stack_right(right))
        q_buf[:, columns] = q_new
        out_buf[:, columns] = merged_ref[:, columns] - dot(basis_ref[...], stack_right(q_new))
        for which, (buf, ref) in enumerate(((out_buf, out_ref), (q_buf, q_ref))):
            copies.append(pltpu.make_async_copy(buf.at[:, columns], ref.at[:, columns], sems.at[which, half]))
            copies[-1].start()
    for copy in copies:
        copy.wait()


def final(*operands):
    return kernel_call(
        final_body,
        (shape(ROWS, WIDTH), shape(RANK, WIDTH)),
        in_specs=[VMEM] * 4,
        out_specs=(ANY, ANY),
        scratch_shapes=[
            pltpu.VMEM((ROWS, WIDTH), F32),
            pltpu.VMEM((RANK, WIDTH), F32),
            pltpu.SemaphoreType.DMA((2, 2)),
        ],
    )(*(pltpu.with_memory_space_constraint(value, pltpu.VMEM) for value in operands))


def exchange(values, groups):
    return lax.all_to_all(values, AXES, 0, 0, axis_index_groups=groups)


def spread(value, groups):
    return exchange(jnp.broadcast_to(value[None], (len(groups[0]),) + value.shape), groups)


def both_cores(value):
    return lax.all_gather(value, AXES, axis_index_groups=CHIP_GROUPS)


def per_device(grad, error, q_prev):
    replicas = lax.axis_size("dp")
    dp = lax.axis_index("dp").astype(jnp.uint32)
    core = dp % 2
    row = lax.broadcasted_iota(jnp.uint32, (16, LANES), 0)
    place = jnp.where(row < 8, row == dp // 2, core == 1).astype(F32)

    p_local, merged = left_product(grad[0], error[0], q_prev.T)
    p_both, halves, core = lax.optimization_barrier((both_cores(p_local), merged, core))
    given = lax.dynamic_slice_in_dim(halves, (1 - core) * HALF, HALF, axis=1)
    own_half = lax.dynamic_slice_in_dim(halves, core * HALF, HALF, axis=1)
    taken = lax.ppermute(given, AXES, CORE_SWAP)
    p_parts = spread(jnp.sum(p_both, axis=0), Y_GROUPS)
    p_sum, p_split, row = vmem_call(
        parts_body,
        (in_vmem(RANK, ROWS), in_vmem(3 * RANK, ROWS, dtype=BF16), in_vmem(8, LANES)),
        cost_estimate=pl.CostEstimate(flops=COST, bytes_accessed=COST, transcendentals=0),
    )(place, p_parts)
    pieces = exchange(right_product(p_split, row, own_half, taken), PLANE_GROUPS)
    lines = vmem_call(plane_body, in_vmem(RING, PIECE + 8, LANES))(place, pieces)
    lines = exchange(lines, LINE_GROUPS)
    own = vmem_call(line_body, in_vmem(PLANE, PIECE, LANES))(lines)
    own = exchange(own, PLANE_GROUPS)
    basis, basis_stack, inverse_stack = vmem_call(
        functools.partial(factor_body, replicas),
        (shape(RANK, ROWS), in_vmem(ROWS, 6 * RANK, dtype=BF16), in_vmem(RANK, 6 * RANK, dtype=BF16)),
    )(lines, p_sum)
    whole = both_cores(own)
    new_error, q_new = final(whole, inverse_stack, basis_stack, merged)
    return (new_error[None], basis.T, q_new.T)


def solution(mesh):
    placed = (P("dp", "vocab", None), P("dp", "vocab", None), P())
    return jax.shard_map(
        per_device,
        mesh=mesh,
        in_specs=placed,
        out_specs=(P("dp", "vocab", None), P("vocab", None), P()),
        check_vma=False,
    )
```

```python
import functools

import jax
import jax.numpy as jnp
from jax import lax
from jax.experimental import pallas as pl
from jax.experimental.pallas import tpu as pltpu
from jax.sharding import PartitionSpec as P

F32, BF16 = jnp.float32, jnp.bfloat16
HIGHEST = lax.Precision.HIGHEST
AXES = ("dp", "vocab")
RING, NX = 8, 4
PLANE = RING * NX


def device(y, core, z, x):
    return ((y * 2 + core) * RING + z) * NX + x


FAR_FIRST = (0, 4, 1, 5, 2, 6, 3, 7)
X_ORDER = (0, 2, 1, 3)
CHIP_GROUPS = [[device(y, c, z, x) for c in range(2)] for y in range(RING) for z in range(RING) for x in range(NX)]
Y_GROUPS = [[device(y, c, z, x) for y in FAR_FIRST] for c in range(2) for z in range(RING) for x in range(NX)]


def across(core, a, b, x):
    return device(a, core, b, x) if core else device(b, core, a, x)


PLANE_GROUPS = [
    [across(c, a, b, x) for x in X_ORDER for a in range(RING)] for c in range(2) for b in range(RING)
]
LINE_GROUPS = [
    [across(c, a, b, x) for b in FAR_FIRST] for c in range(2) for a in range(RING) for x in range(NX)
]
RANK, ROWS, WIDTH = 32, 128, 3584
HALF = WIDTH // 2
LANES = 128
TILES = HALF // LANES
PIECE = TILES + 2
VMEM_LIMIT = 48 * 1024 * 1024
LEFT_CHUNKS = (1024, 1024, 1024, 512)
ANY = pl.BlockSpec(memory_space=pl.ANY)
VMEM = pl.BlockSpec(memory_space=pltpu.VMEM)

NT = (((1,), (1,)), ((), ()))
NN = (((1,), (0,)), ((), ()))


def split3(value):
    high = value.astype(BF16)
    rest = value - high.astype(F32)
    middle = rest.astype(BF16)
    low = (rest - middle.astype(F32)).astype(BF16)
    return high, middle, low


def dot(a, b, dims=NN):
    return lax.dot_general(a, b, dims, preferred_element_type=F32)


def stack_left(value):
    h, m, l = split3(value)
    return jnp.concatenate([h, h, m, m, h, l], axis=1)


def stack_right(value):
    h, m, l = split3(value)
    return jnp.concatenate([h, m, h, m, l, h], axis=0)


def kernel_call(body, out_shape, **options):
    return pl.pallas_call(
        body,
        out_shape=out_shape,
        compiler_params=pltpu.CompilerParams(vmem_limit_bytes=VMEM_LIMIT),
        **options,
    )


def vmem_call(body, out_shape):
    def call(*operands):
        return kernel_call(body, out_shape)(
            *(pltpu.with_memory_space_constraint(value, pltpu.VMEM) for value in operands)
        )

    return call


def shape(*dims):
    return jax.ShapeDtypeStruct(dims, F32)


def in_vmem(*dims, dtype=F32):
    return pltpu.VMEM(dims, dtype)


def left_body(grad_ref, error_ref, q_ref, p_ref, merged_ref, grad_buf, error_buf, q_buf, sems):
    plan, start = [], 0
    for at, size in enumerate(LEFT_CHUNKS):
        columns = pl.ds(start, size)
        copies = [
            pltpu.make_async_copy(ref.at[:, columns], buf.at[:, columns], sems.at[which, at])
            for which, (ref, buf) in enumerate(((grad_ref, grad_buf), (error_ref, error_buf), (q_ref, q_buf)))
        ]
        for copy in copies:
            copy.start()
        plan.append((slice(start, start + size), copies))
        start += size
    total = None
    for columns, copies in plan:
        for copy in copies:
            copy.wait()
        merged = grad_buf[:, columns].astype(F32) + error_buf[:, columns]
        merged_ref[:, columns] = merged
        left = jnp.concatenate(split3(q_buf[:, columns]), axis=0)
        right = jnp.concatenate(split3(merged), axis=0)
        product = dot(left, right, NT)
        total = product if total is None else total + product
    total = total[:RANK] + (total[RANK : 2 * RANK] + total[2 * RANK :])
    p_ref[...] = total[:, :ROWS] + (total[:, ROWS : 2 * ROWS] + total[:, 2 * ROWS :])


def left_product(grad, error, q_rows):
    return kernel_call(
        left_body,
        (in_vmem(RANK, ROWS), in_vmem(ROWS, WIDTH)),
        in_specs=[ANY] * 3,
        out_specs=(VMEM, VMEM),
        scratch_shapes=[
            pltpu.VMEM((ROWS, WIDTH), BF16),
            pltpu.VMEM((ROWS, WIDTH), F32),
            pltpu.VMEM((RANK, WIDTH), F32),
            pltpu.SemaphoreType.DMA((3, len(LEFT_CHUNKS))),
        ],
    )(*(pltpu.with_memory_space_constraint(value, pltpu.HBM) for value in (grad, error, q_rows)))


def right_body(place_ref, parts_ref, merged_ref, pieces_ref, p_ref):
    p_sum = jnp.sum(parts_ref[...], axis=0)
    p_ref[...] = p_sum
    p_parts = jnp.concatenate(split3(p_sum), axis=0)
    gram = lax.dot_general(p_sum, p_sum, NT, precision=HIGHEST, preferred_element_type=F32)
    packed = jnp.concatenate([gram[8 * a : 8 * a + 8] for a in range(4)], axis=1)
    row = 0.5 * jnp.sum(packed * place_ref[:8, :], axis=0, keepdims=True)
    for half in range(2):
        h, m, l = split3(merged_ref[:, half * HALF : (half + 1) * HALF])
        with_h = dot(p_parts, h)
        with_m = dot(p_parts[: 2 * RANK], m)
        with_l = dot(p_parts[:RANK], l)
        small = with_h[2 * RANK :] + with_m[RANK:] + with_l
        product = with_h[:RANK] + (with_h[RANK : 2 * RANK] + with_m[:RANK] + small)
        for tile in range(TILES):
            pieces_ref[half, :, tile, :] = product[:, tile * LANES : (tile + 1) * LANES]
        pieces_ref[half, :, TILES, :] = jnp.broadcast_to(row, (RANK, LANES))
        pieces_ref[half, :, TILES + 1, :] = jnp.zeros((RANK, LANES), F32)


def right_product(place, parts, merged):
    return vmem_call(right_body, (in_vmem(2, RANK, PIECE, LANES), in_vmem(RANK, ROWS)))(place, parts, merged)


def plane_body(place_ref, parts_ref, out_ref):
    rows = parts_ref[0]
    for member in range(1, PLANE):
        rows += parts_ref[member]
    apart = [sum(parts_ref[x * RING + a, TILES : TILES + 1, :] for x in range(NX)) for a in range(RING)]
    total = apart[FAR_FIRST[0]]
    for z in FAR_FIRST[1:]:
        total += apart[z]
    gram = jnp.where(place_ref[8:, :] > 0, total * place_ref[:8, :], jnp.concatenate(apart, axis=0))
    both = jnp.concatenate([rows, gram], axis=0)
    for member in range(RING):
        out_ref[member] = both


def line_body(parts_ref, out_ref):
    rows = parts_ref[0, :PIECE, :]
    for member in range(1, RING):
        rows += parts_ref[member, :PIECE, :]
    for member in range(PLANE):
        out_ref[member] = rows


def factor_body(replicas, parts_ref, p_ref, basis_ref, basis_stack_ref, inverse_stack_ref):
    packed = parts_ref[0, PIECE:, :]
    for member in range(1, RING):
        packed += parts_ref[member, PIECE:, :]
    gram = jnp.concatenate([packed[:, RANK * a : RANK * (a + 1)] for a in range(4)], axis=0)
    row = lax.broadcasted_iota(jnp.int32, (RANK, RANK), 0)
    column = lax.broadcasted_iota(jnp.int32, (RANK, RANK), 1)
    unit = jnp.where(row == column, 1.0, 0.0).astype(F32)
    work = jnp.concatenate([gram, unit], axis=1)
    below = lax.broadcasted_iota(jnp.int32, (RANK, 1), 0)
    inverse = []
    for j in range(RANK):
        pivot_row = work[j : j + 1, :]
        pivot = pivot_row[:, j : j + 1]
        inverse.append(pivot_row[:, RANK:] / jnp.sqrt(pivot))
        if j < RANK - 1:
            factor = jnp.where(below > j, work[:, j : j + 1] / pivot, 0.0)
            work = work - factor * pivot_row
    inverse = jnp.concatenate(inverse, axis=0)
    basis = lax.dot_general(inverse, p_ref[...], NN, precision=HIGHEST, preferred_element_type=F32)
    basis_ref[...] = basis
    basis_stack_ref[...] = stack_left(basis.T)
    inverse_stack_ref[...] = stack_left(inverse * (1.0 / replicas))


def final_body(parts_ref, inverse_ref, basis_ref, merged_ref, out_ref, q_ref, out_buf, q_buf, sems):
    copies = []
    for half in range(2):
        right = jnp.concatenate([parts_ref[half, :, tile, :] for tile in range(TILES)], axis=1)
        columns = slice(half * HALF, (half + 1) * HALF)
        q_new = dot(inverse_ref[...], stack_right(right))
        q_buf[:, columns] = q_new
        out_buf[:, columns] = merged_ref[:, columns] - dot(basis_ref[...], stack_right(q_new))
        for which, (buf, ref) in enumerate(((out_buf, out_ref), (q_buf, q_ref))):
            copies.append(pltpu.make_async_copy(buf.at[:, columns], ref.at[:, columns], sems.at[which, half]))
            copies[-1].start()
    for copy in copies:
        copy.wait()


def final(*operands):
    return kernel_call(
        final_body,
        (shape(ROWS, WIDTH), shape(RANK, WIDTH)),
        in_specs=[VMEM] * 4,
        out_specs=(ANY, ANY),
        scratch_shapes=[
            pltpu.VMEM((ROWS, WIDTH), F32),
            pltpu.VMEM((RANK, WIDTH), F32),
            pltpu.SemaphoreType.DMA((2, 2)),
        ],
    )(*(pltpu.with_memory_space_constraint(value, pltpu.VMEM) for value in operands))


def pick(values, at):
    return lax.dynamic_index_in_dim(values, at, keepdims=False)


def exchange(values, groups):
    return lax.all_to_all(values, AXES, 0, 0, axis_index_groups=groups)


def spread(value, groups):
    return exchange(jnp.broadcast_to(value[None], (len(groups[0]),) + value.shape), groups)


def both_cores(value):
    return lax.all_gather(value, AXES, axis_index_groups=CHIP_GROUPS)


def per_device(grad, error, q_prev):
    replicas = lax.axis_size("dp")
    dp = lax.axis_index("dp").astype(jnp.uint32)
    core = dp % 2
    row = lax.broadcasted_iota(jnp.uint32, (16, LANES), 0)
    place = jnp.where(row < 8, row == dp // 2, core == 0).astype(F32)

    p_local, merged = left_product(grad[0], error[0], q_prev.T)
    p_both, place, core, other = lax.optimization_barrier((both_cores(p_local), place, core, 1 - core))
    p_parts = spread(jnp.sum(p_both, axis=0), Y_GROUPS)

    pieces, p_sum = right_product(place, p_parts, merged)
    traded = both_cores(pick(pieces, other))
    pieces = exchange(pick(pieces, core) + pick(traded, other), PLANE_GROUPS)
    lines = vmem_call(plane_body, in_vmem(RING, PIECE + 8, LANES))(place, pieces)
    lines = exchange(lines, LINE_GROUPS)
    own = vmem_call(line_body, in_vmem(PLANE, PIECE, LANES))(lines)
    own = exchange(own, PLANE_GROUPS)
    basis, basis_stack, inverse_stack = vmem_call(
        functools.partial(factor_body, replicas),
        (shape(RANK, ROWS), in_vmem(ROWS, 6 * RANK, dtype=BF16), in_vmem(RANK, 6 * RANK, dtype=BF16)),
    )(lines, p_sum)
    whole = both_cores(own)
    new_error, q_new = final(whole, inverse_stack, basis_stack, merged)
    return (new_error[None], basis.T, q_new.T)


def solution(mesh):
    placed = (P("dp", "vocab", None), P("dp", "vocab", None), P())
    return jax.shard_map(
        per_device,
        mesh=mesh,
        in_specs=placed,
        out_specs=(P("dp", "vocab", None), P("vocab", None), P()),
        check_vma=False,
    )
```

```python
import functools

import jax
import jax.numpy as jnp
from jax import lax
from jax.experimental import pallas as pl
from jax.experimental.pallas import tpu as pltpu
from jax.sharding import PartitionSpec as P

F32, BF16 = jnp.float32, jnp.bfloat16
HIGHEST = lax.Precision.HIGHEST
AXES = ("dp", "vocab")
RING, NX = 8, 4
PLANE = RING * NX


def device(y, core, z, x):
    return ((y * 2 + core) * RING + z) * NX + x


FAR_FIRST = (0, 4, 1, 5, 2, 6, 3, 7)
X_ORDER = (0, 2, 1, 3)
CHIP_GROUPS = [[device(y, c, z, x) for c in range(2)] for y in range(RING) for z in range(RING) for x in range(NX)]
Y_GROUPS = [[device(y, c, z, x) for y in FAR_FIRST] for c in range(2) for z in range(RING) for x in range(NX)]


def across(core, a, b, x):
    return device(a, core, b, x) if core else device(b, core, a, x)


PLANE_GROUPS = [
    [across(c, a, b, x) for x in X_ORDER for a in range(RING)] for c in range(2) for b in range(RING)
]
LINE_GROUPS = [
    [across(c, a, b, x) for b in FAR_FIRST] for c in range(2) for a in range(RING) for x in range(NX)
]
RANK, ROWS, WIDTH = 32, 128, 3584
HALF = WIDTH // 2
LANES = 128
TILES = HALF // LANES
PIECE = TILES + 2
VMEM_LIMIT = 48 * 1024 * 1024
LEFT_CHUNKS = (1024, 1024, 1024, 512)
ANY = pl.BlockSpec(memory_space=pl.ANY)
VMEM = pl.BlockSpec(memory_space=pltpu.VMEM)

NT = (((1,), (1,)), ((), ()))
NN = (((1,), (0,)), ((), ()))


def split3(value):
    high = value.astype(BF16)
    rest = value - high.astype(F32)
    middle = rest.astype(BF16)
    low = (rest - middle.astype(F32)).astype(BF16)
    return high, middle, low


def dot(a, b, dims=NN):
    return lax.dot_general(a, b, dims, preferred_element_type=F32)


def stack_left(value):
    h, m, l = split3(value)
    return jnp.concatenate([h, h, m, m, h, l], axis=1)


def stack_right(value):
    h, m, l = split3(value)
    return jnp.concatenate([h, m, h, m, l, h], axis=0)


def kernel_call(body, out_shape, **options):
    return pl.pallas_call(
        body,
        out_shape=out_shape,
        compiler_params=pltpu.CompilerParams(vmem_limit_bytes=VMEM_LIMIT),
        **options,
    )


def vmem_call(body, out_shape):
    def call(*operands):
        return kernel_call(body, out_shape)(
            *(pltpu.with_memory_space_constraint(value, pltpu.VMEM) for value in operands)
        )

    return call


def shape(*dims):
    return jax.ShapeDtypeStruct(dims, F32)


def in_vmem(*dims, dtype=F32):
    return pltpu.VMEM(dims, dtype)


def left_body(grad_ref, error_ref, q_ref, p_ref, merged_ref, grad_buf, error_buf, q_buf, sems):
    plan, start = [], 0
    for at, size in enumerate(LEFT_CHUNKS):
        columns = pl.ds(start, size)
        copies = [
            pltpu.make_async_copy(ref.at[:, columns], buf.at[:, columns], sems.at[which, at])
            for which, (ref, buf) in enumerate(((grad_ref, grad_buf), (error_ref, error_buf), (q_ref, q_buf)))
        ]
        for copy in copies:
            copy.start()
        plan.append((slice(start, start + size), copies))
        start += size
    total = None
    for columns, copies in plan:
        for copy in copies:
            copy.wait()
        merged = grad_buf[:, columns].astype(F32) + error_buf[:, columns]
        merged_ref[:, columns] = merged
        left = jnp.concatenate(split3(q_buf[:, columns]), axis=0)
        right = jnp.concatenate(split3(merged), axis=0)
        product = dot(left, right, NT)
        total = product if total is None else total + product
    total = total[:RANK] + (total[RANK : 2 * RANK] + total[2 * RANK :])
    p_ref[...] = total[:, :ROWS] + (total[:, ROWS : 2 * ROWS] + total[:, 2 * ROWS :])


def left_product(grad, error, q_rows):
    return kernel_call(
        left_body,
        (in_vmem(RANK, ROWS), in_vmem(ROWS, WIDTH)),
        in_specs=[ANY] * 3,
        out_specs=(VMEM, VMEM),
        scratch_shapes=[
            pltpu.VMEM((ROWS, WIDTH), BF16),
            pltpu.VMEM((ROWS, WIDTH), F32),
            pltpu.VMEM((RANK, WIDTH), F32),
            pltpu.SemaphoreType.DMA((3, len(LEFT_CHUNKS))),
        ],
    )(*(pltpu.with_memory_space_constraint(value, pltpu.HBM) for value in (grad, error, q_rows)))


def one_row(rows):
    return (lax.broadcasted_iota(jnp.int32, (rows, LANES), 0) == lax.axis_index("dp") // 2).astype(F32)


def right_body(parts_ref, merged_ref, own_ref, given_ref, p_ref):
    core = lax.axis_index("dp") % 2
    p_sum = jnp.sum(parts_ref[...], axis=0)
    p_ref[...] = p_sum
    p_parts = jnp.concatenate(split3(p_sum), axis=0)
    gram = lax.dot_general(p_sum, p_sum, NT, precision=HIGHEST, preferred_element_type=F32)
    packed = jnp.concatenate([gram[8 * a : 8 * a + 8] for a in range(4)], axis=1)
    row = jnp.broadcast_to(0.5 * jnp.sum(packed * one_row(8), axis=0, keepdims=True), (RANK, LANES))

    def store(ref, product):
        for tile in range(TILES):
            ref[:, tile, :] = product[:, tile * LANES : (tile + 1) * LANES]
        ref[:, TILES, :] = row
        ref[:, TILES + 1, :] = jnp.zeros((RANK, LANES), F32)

    for half in range(2):
        h, m, l = split3(merged_ref[:, half * HALF : (half + 1) * HALF])
        with_h = dot(p_parts, h)
        with_m = dot(p_parts[: 2 * RANK], m)
        with_l = dot(p_parts[:RANK], l)
        small = with_h[2 * RANK :] + with_m[RANK:] + with_l
        product = with_h[:RANK] + (with_h[RANK : 2 * RANK] + with_m[:RANK] + small)
        pl.when(core == half)(functools.partial(store, own_ref, product))
        pl.when(core != half)(functools.partial(store, given_ref, product))


def right_product(parts, merged):
    pieces = in_vmem(RANK, PIECE, LANES)
    return vmem_call(right_body, (pieces, pieces, in_vmem(RANK, ROWS)))(parts, merged)


def plane_body(parts_ref, out_ref):
    rows = parts_ref[0]
    for member in range(1, PLANE):
        rows += parts_ref[member]
    apart = [sum(parts_ref[x * RING + a, TILES : TILES + 1, :] for x in range(NX)) for a in range(RING)]
    total = apart[FAR_FIRST[0]]
    for z in FAR_FIRST[1:]:
        total += apart[z]
    gram = jnp.where(lax.axis_index("dp") % 2 == 0, total * one_row(8), jnp.concatenate(apart, axis=0))
    both = jnp.concatenate([rows, gram], axis=0)
    for member in range(RING):
        out_ref[member] = both


def line_body(parts_ref, out_ref):
    rows = parts_ref[0, :PIECE, :]
    for member in range(1, RING):
        rows += parts_ref[member, :PIECE, :]
    for member in range(PLANE):
        out_ref[member] = rows


def factor_body(replicas, parts_ref, p_ref, basis_ref, basis_stack_ref, inverse_stack_ref):
    packed = parts_ref[0, PIECE:, :]
    for member in range(1, RING):
        packed += parts_ref[member, PIECE:, :]
    gram = jnp.concatenate([packed[:, RANK * a : RANK * (a + 1)] for a in range(4)], axis=0)
    row = lax.broadcasted_iota(jnp.int32, (RANK, RANK), 0)
    column = lax.broadcasted_iota(jnp.int32, (RANK, RANK), 1)
    unit = jnp.where(row == column, 1.0, 0.0).astype(F32)
    work = jnp.concatenate([gram, unit], axis=1)
    below = lax.broadcasted_iota(jnp.int32, (RANK, 1), 0)
    inverse = []
    for j in range(RANK):
        pivot_row = work[j : j + 1, :]
        pivot = pivot_row[:, j : j + 1]
        inverse.append(pivot_row[:, RANK:] / jnp.sqrt(pivot))
        if j < RANK - 1:
            factor = jnp.where(below > j, work[:, j : j + 1] / pivot, 0.0)
            work = work - factor * pivot_row
    inverse = jnp.concatenate(inverse, axis=0)
    basis = lax.dot_general(inverse, p_ref[...], NN, precision=HIGHEST, preferred_element_type=F32)
    basis_ref[...] = basis
    basis_stack_ref[...] = stack_left(basis.T)
    inverse_stack_ref[...] = stack_left(inverse * (1.0 / replicas))


def final_body(parts_ref, inverse_ref, basis_ref, merged_ref, out_ref, q_ref, out_buf, q_buf, sems):
    copies = []
    for half in range(2):
        right = jnp.concatenate([parts_ref[half, :, tile, :] for tile in range(TILES)], axis=1)
        columns = slice(half * HALF, (half + 1) * HALF)
        q_new = dot(inverse_ref[...], stack_right(right))
        q_buf[:, columns] = q_new
        out_buf[:, columns] = merged_ref[:, columns] - dot(basis_ref[...], stack_right(q_new))
        for which, (buf, ref) in enumerate(((out_buf, out_ref), (q_buf, q_ref))):
            copies.append(pltpu.make_async_copy(buf.at[:, columns], ref.at[:, columns], sems.at[which, half]))
            copies[-1].start()
    for copy in copies:
        copy.wait()


def final(*operands):
    return kernel_call(
        final_body,
        (shape(ROWS, WIDTH), shape(RANK, WIDTH)),
        in_specs=[VMEM] * 4,
        out_specs=(ANY, ANY),
        scratch_shapes=[
            pltpu.VMEM((ROWS, WIDTH), F32),
            pltpu.VMEM((RANK, WIDTH), F32),
            pltpu.SemaphoreType.DMA((2, 2)),
        ],
    )(*(pltpu.with_memory_space_constraint(value, pltpu.VMEM) for value in operands))


def exchange(values, groups):
    return lax.all_to_all(values, AXES, 0, 0, axis_index_groups=groups)


def spread(value, groups):
    return exchange(jnp.broadcast_to(value[None], (len(groups[0]),) + value.shape), groups)


def both_cores(value):
    return lax.all_gather(value, AXES, axis_index_groups=CHIP_GROUPS)


def per_device(grad, error, q_prev):
    replicas = lax.axis_size("dp")
    other = 1 - lax.axis_index("dp").astype(jnp.uint32) % 2

    p_local, merged = left_product(grad[0], error[0], q_prev.T)
    p_both, other = lax.optimization_barrier((both_cores(p_local), other))
    p_parts = spread(jnp.sum(p_both, axis=0), Y_GROUPS)

    pieces, given, p_sum = right_product(p_parts, merged)
    pieces += lax.dynamic_index_in_dim(both_cores(given), other, keepdims=False)
    pieces = exchange(pieces, PLANE_GROUPS)
    lines = vmem_call(plane_body, in_vmem(RING, PIECE + 8, LANES))(pieces)
    lines = exchange(lines, LINE_GROUPS)
    own = vmem_call(line_body, in_vmem(PLANE, PIECE, LANES))(lines)
    own = exchange(own, PLANE_GROUPS)
    basis, basis_stack, inverse_stack = vmem_call(
        functools.partial(factor_body, replicas),
        (shape(RANK, ROWS), in_vmem(ROWS, 6 * RANK, dtype=BF16), in_vmem(RANK, 6 * RANK, dtype=BF16)),
    )(lines, p_sum)
    whole = both_cores(own)
    new_error, q_new = final(whole, inverse_stack, basis_stack, merged)
    return (new_error[None], basis.T, q_new.T)


def solution(mesh):
    placed = (P("dp", "vocab", None), P("dp", "vocab", None), P())
    return jax.shard_map(
        per_device,
        mesh=mesh,
        in_specs=placed,
        out_specs=(P("dp", "vocab", None), P("vocab", None), P()),
        check_vma=False,
    )
```

```python
import functools

import jax
import jax.numpy as jnp
from jax import lax
from jax.experimental import pallas as pl
from jax.experimental.pallas import tpu as pltpu
from jax.sharding import PartitionSpec as P

F32, BF16 = jnp.float32, jnp.bfloat16
HIGHEST = lax.Precision.HIGHEST
AXES = ("dp", "vocab")
RING, NX = 8, 4
PLANE = RING * NX


def device(y, core, z, x):
    return ((y * 2 + core) * RING + z) * NX + x


FAR_FIRST = (0, 4, 1, 5, 2, 6, 3, 7)
X_ORDER = (0, 2, 1, 3)
CHIP_GROUPS = [[device(y, c, z, x) for c in range(2)] for y in range(RING) for z in range(RING) for x in range(NX)]
Y_GROUPS = [[device(y, c, z, x) for y in FAR_FIRST] for c in range(2) for z in range(RING) for x in range(NX)]


def across(core, a, b, x):
    return device(a, core, b, x) if core else device(b, core, a, x)


PLANE_GROUPS = [
    [across(c, a, b, x) for x in X_ORDER for a in range(RING)] for c in range(2) for b in range(RING)
]
LINE_GROUPS = [
    [across(c, a, b, x) for b in FAR_FIRST] for c in range(2) for a in range(RING) for x in range(NX)
]
RANK, ROWS, WIDTH = 32, 128, 3584
HALF = WIDTH // 2
LANES = 128
TILES = HALF // LANES
PIECE = TILES + 2
VMEM_LIMIT = 48 * 1024 * 1024
LEFT_CHUNKS = (1024, 1024, 1024, 512)
ANY = pl.BlockSpec(memory_space=pl.ANY)
VMEM = pl.BlockSpec(memory_space=pltpu.VMEM)

NT = (((1,), (1,)), ((), ()))
NN = (((1,), (0,)), ((), ()))


def split3(value):
    high = value.astype(BF16)
    rest = value - high.astype(F32)
    middle = rest.astype(BF16)
    low = (rest - middle.astype(F32)).astype(BF16)
    return high, middle, low


def dot(a, b, dims=NN):
    return lax.dot_general(a, b, dims, preferred_element_type=F32)


def stack_left(value):
    h, m, l = split3(value)
    return jnp.concatenate([h, h, m, m, h, l], axis=1)


def stack_right(value):
    h, m, l = split3(value)
    return jnp.concatenate([h, m, h, m, l, h], axis=0)


def kernel_call(body, out_shape, **options):
    return pl.pallas_call(
        body,
        out_shape=out_shape,
        compiler_params=pltpu.CompilerParams(vmem_limit_bytes=VMEM_LIMIT),
        **options,
    )


def vmem_call(body, out_shape):
    def call(*operands):
        return kernel_call(body, out_shape)(
            *(pltpu.with_memory_space_constraint(value, pltpu.VMEM) for value in operands)
        )

    return call


def shape(*dims):
    return jax.ShapeDtypeStruct(dims, F32)


def in_vmem(*dims, dtype=F32):
    return pltpu.VMEM(dims, dtype)


def left_body(grad_ref, error_ref, q_ref, p_ref, merged_ref, grad_buf, error_buf, q_buf, sems):
    plan, start = [], 0
    for at, size in enumerate(LEFT_CHUNKS):
        columns = pl.ds(start, size)
        copies = [
            pltpu.make_async_copy(ref.at[:, columns], buf.at[:, columns], sems.at[which, at])
            for which, (ref, buf) in enumerate(((grad_ref, grad_buf), (error_ref, error_buf), (q_ref, q_buf)))
        ]
        for copy in copies:
            copy.start()
        plan.append((slice(start, start + size), copies))
        start += size
    total = None
    for columns, copies in plan:
        for copy in copies:
            copy.wait()
        merged = grad_buf[:, columns].astype(F32) + error_buf[:, columns]
        merged_ref[:, columns] = merged
        left = jnp.concatenate(split3(q_buf[:, columns]), axis=0)
        right = jnp.concatenate(split3(merged), axis=0)
        product = dot(left, right, NT)
        total = product if total is None else total + product
    total = total[:RANK] + (total[RANK : 2 * RANK] + total[2 * RANK :])
    p_ref[...] = total[:, :ROWS] + (total[:, ROWS : 2 * ROWS] + total[:, 2 * ROWS :])


def left_product(grad, error, q_rows):
    return kernel_call(
        left_body,
        (in_vmem(RANK, ROWS), in_vmem(ROWS, WIDTH)),
        in_specs=[ANY] * 3,
        out_specs=(VMEM, VMEM),
        scratch_shapes=[
            pltpu.VMEM((ROWS, WIDTH), BF16),
            pltpu.VMEM((ROWS, WIDTH), F32),
            pltpu.VMEM((RANK, WIDTH), F32),
            pltpu.SemaphoreType.DMA((3, len(LEFT_CHUNKS))),
        ],
    )(*(pltpu.with_memory_space_constraint(value, pltpu.HBM) for value in (grad, error, q_rows)))


def right_body(place_ref, parts_ref, merged_ref, pieces_ref, p_ref):
    p_sum = jnp.sum(parts_ref[...], axis=0)
    p_ref[...] = p_sum
    p_parts = jnp.concatenate(split3(p_sum), axis=0)
    gram = lax.dot_general(p_sum, p_sum, NT, precision=HIGHEST, preferred_element_type=F32)
    packed = jnp.concatenate([gram[8 * a : 8 * a + 8] for a in range(4)], axis=1)
    row = 0.5 * jnp.sum(packed * place_ref[:8, :], axis=0, keepdims=True)
    for half in range(2):
        h, m, l = split3(merged_ref[:, half * HALF : (half + 1) * HALF])
        with_h = dot(p_parts, h)
        with_m = dot(p_parts[: 2 * RANK], m)
        with_l = dot(p_parts[:RANK], l)
        small = with_h[2 * RANK :] + with_m[RANK:] + with_l
        product = with_h[:RANK] + (with_h[RANK : 2 * RANK] + with_m[:RANK] + small)
        for tile in range(TILES):
            pieces_ref[half, :, tile, :] = product[:, tile * LANES : (tile + 1) * LANES]
        pieces_ref[half, :, TILES, :] = jnp.broadcast_to(row, (RANK, LANES))
        pieces_ref[half, :, TILES + 1, :] = jnp.zeros((RANK, LANES), F32)


def right_product(place, parts, merged):
    return vmem_call(right_body, (in_vmem(2, RANK, PIECE, LANES), in_vmem(RANK, ROWS)))(place, parts, merged)


def plane_body(place_ref, parts_ref, out_ref):
    rows = parts_ref[0]
    for member in range(1, PLANE):
        rows += parts_ref[member]
    apart = [sum(parts_ref[x * RING + a, TILES : TILES + 1, :] for x in range(NX)) for a in range(RING)]
    total = apart[FAR_FIRST[0]]
    for z in FAR_FIRST[1:]:
        total += apart[z]
    gram = jnp.where(place_ref[8:, :] > 0, total * place_ref[:8, :], jnp.concatenate(apart, axis=0))
    both = jnp.concatenate([rows, gram], axis=0)
    for member in range(RING):
        out_ref[member] = both


def line_body(parts_ref, out_ref):
    rows = parts_ref[0, :PIECE, :]
    for member in range(1, RING):
        rows += parts_ref[member, :PIECE, :]
    for member in range(PLANE):
        out_ref[member] = rows


def factor_body(replicas, parts_ref, p_ref, basis_ref, basis_stack_ref, inverse_stack_ref):
    packed = parts_ref[0, PIECE:, :]
    for member in range(1, RING):
        packed += parts_ref[member, PIECE:, :]
    gram = jnp.concatenate([packed[:, RANK * a : RANK * (a + 1)] for a in range(4)], axis=0)
    row = lax.broadcasted_iota(jnp.int32, (RANK, RANK), 0)
    column = lax.broadcasted_iota(jnp.int32, (RANK, RANK), 1)
    unit = jnp.where(row == column, 1.0, 0.0).astype(F32)
    work = jnp.concatenate([gram, unit], axis=1)
    below = lax.broadcasted_iota(jnp.int32, (RANK, 1), 0)
    inverse = []
    for j in range(RANK):
        pivot_row = work[j : j + 1, :]
        pivot = pivot_row[:, j : j + 1]
        inverse.append(pivot_row[:, RANK:] / jnp.sqrt(pivot))
        if j < RANK - 1:
            factor = jnp.where(below > j, work[:, j : j + 1] / pivot, 0.0)
            work = work - factor * pivot_row
    inverse = jnp.concatenate(inverse, axis=0)
    basis = lax.dot_general(inverse, p_ref[...], NN, precision=HIGHEST, preferred_element_type=F32)
    basis_ref[...] = basis
    basis_stack_ref[...] = stack_left(basis.T)
    inverse_stack_ref[...] = stack_left(inverse * (1.0 / replicas))


def final_body(parts_ref, inverse_ref, basis_ref, merged_ref, out_ref, q_ref, out_buf, q_buf, sems):
    copies = []
    for half in range(2):
        right = jnp.concatenate([parts_ref[half, :, tile, :] for tile in range(TILES)], axis=1)
        columns = slice(half * HALF, (half + 1) * HALF)
        q_new = dot(inverse_ref[...], stack_right(right))
        q_buf[:, columns] = q_new
        out_buf[:, columns] = merged_ref[:, columns] - dot(basis_ref[...], stack_right(q_new))
        for which, (buf, ref) in enumerate(((out_buf, out_ref), (q_buf, q_ref))):
            copies.append(pltpu.make_async_copy(buf.at[:, columns], ref.at[:, columns], sems.at[which, half]))
            copies[-1].start()
    for copy in copies:
        copy.wait()


def final(*operands):
    return kernel_call(
        final_body,
        (shape(ROWS, WIDTH), shape(RANK, WIDTH)),
        in_specs=[VMEM] * 4,
        out_specs=(ANY, ANY),
        scratch_shapes=[
            pltpu.VMEM((ROWS, WIDTH), F32),
            pltpu.VMEM((RANK, WIDTH), F32),
            pltpu.SemaphoreType.DMA((2, 2)),
        ],
    )(*(pltpu.with_memory_space_constraint(value, pltpu.VMEM) for value in operands))


def pick(values, at):
    return lax.dynamic_index_in_dim(values, at, keepdims=False)


def exchange(values, groups):
    return lax.all_to_all(values, AXES, 0, 0, axis_index_groups=groups)


def spread(value, groups):
    return exchange(jnp.broadcast_to(value[None], (len(groups[0]),) + value.shape), groups)


def both_cores(value):
    return lax.all_gather(value, AXES, axis_index_groups=CHIP_GROUPS)


def per_device(grad, error, q_prev):
    replicas = lax.axis_size("dp")
    dp = lax.axis_index("dp").astype(jnp.uint32)
    core = dp % 2
    row = lax.broadcasted_iota(jnp.uint32, (16, LANES), 0)
    place = jnp.where(row < 8, row == dp // 2, core == 0).astype(F32)

    p_local, merged = left_product(grad[0], error[0], q_prev.T)
    p_local, place, core, other = lax.optimization_barrier((p_local, place, core, 1 - core))
    p_parts = both_cores(jnp.sum(spread(p_local, Y_GROUPS), axis=0))

    pieces, p_sum = right_product(place, p_parts, merged)
    traded = both_cores(pick(pieces, other))
    pieces = exchange(pick(pieces, core) + pick(traded, other), PLANE_GROUPS)
    lines = vmem_call(plane_body, in_vmem(RING, PIECE + 8, LANES))(place, pieces)
    lines = exchange(lines, LINE_GROUPS)
    own = vmem_call(line_body, in_vmem(PLANE, PIECE, LANES))(lines)
    own = exchange(own, PLANE_GROUPS)
    basis, basis_stack, inverse_stack = vmem_call(
        functools.partial(factor_body, replicas),
        (shape(RANK, ROWS), in_vmem(ROWS, 6 * RANK, dtype=BF16), in_vmem(RANK, 6 * RANK, dtype=BF16)),
    )(lines, p_sum)
    whole = both_cores(own)
    new_error, q_new = final(whole, inverse_stack, basis_stack, merged)
    return (new_error[None], basis.T, q_new.T)


def solution(mesh):
    placed = (P("dp", "vocab", None), P("dp", "vocab", None), P())
    return jax.shard_map(
        per_device,
        mesh=mesh,
        in_specs=placed,
        out_specs=(P("dp", "vocab", None), P("vocab", None), P()),
        check_vma=False,
    )
```

```python
import functools

import jax
import jax.numpy as jnp
from jax import lax
from jax.experimental import pallas as pl
from jax.experimental.pallas import tpu as pltpu
from jax.sharding import PartitionSpec as P

F32, BF16 = jnp.float32, jnp.bfloat16
HIGHEST = lax.Precision.HIGHEST
AXES = ("dp", "vocab")
RING, NX = 8, 4
PLANE = RING * NX


def device(y, core, z, x):
    return ((y * 2 + core) * RING + z) * NX + x


FAR_FIRST = (0, 4, 1, 5, 2, 6, 3, 7)
X_ORDER = (0, 2, 1, 3)
CHIP_GROUPS = [[device(y, c, z, x) for c in range(2)] for y in range(RING) for z in range(RING) for x in range(NX)]
Y_GROUPS = [[device(y, c, z, x) for y in FAR_FIRST] for c in range(2) for z in range(RING) for x in range(NX)]


def across(core, a, b, x):
    return device(a, core, b, x) if core else device(b, core, a, x)


PLANE_GROUPS = [
    [across(c, a, b, x) for x in X_ORDER for a in range(RING)] for c in range(2) for b in range(RING)
]
LINE_GROUPS = [
    [across(c, a, b, x) for b in FAR_FIRST] for c in range(2) for a in range(RING) for x in range(NX)
]
RANK, ROWS, WIDTH = 32, 128, 3584
HALF = WIDTH // 2
LANES = 128
TILES = HALF // LANES
PIECE = TILES + 2
VMEM_LIMIT = 48 * 1024 * 1024
LEFT_CHUNKS = (1024, 1024, 1024, 512)
ANY = pl.BlockSpec(memory_space=pl.ANY)
VMEM = pl.BlockSpec(memory_space=pltpu.VMEM)

NT = (((1,), (1,)), ((), ()))
NN = (((1,), (0,)), ((), ()))


def split3(value):
    high = value.astype(BF16)
    rest = value - high.astype(F32)
    middle = rest.astype(BF16)
    low = (rest - middle.astype(F32)).astype(BF16)
    return high, middle, low


def dot(a, b, dims=NN):
    return lax.dot_general(a, b, dims, preferred_element_type=F32)


def stack_left(value):
    h, m, l = split3(value)
    return jnp.concatenate([h, h, m, m, h, l], axis=1)


def stack_right(value):
    h, m, l = split3(value)
    return jnp.concatenate([h, m, h, m, l, h], axis=0)


def kernel_call(body, out_shape, **options):
    return pl.pallas_call(
        body,
        out_shape=out_shape,
        compiler_params=pltpu.CompilerParams(vmem_limit_bytes=VMEM_LIMIT),
        **options,
    )


def vmem_call(body, out_shape):
    def call(*operands):
        return kernel_call(body, out_shape)(
            *(pltpu.with_memory_space_constraint(value, pltpu.VMEM) for value in operands)
        )

    return call


def shape(*dims):
    return jax.ShapeDtypeStruct(dims, F32)


def in_vmem(*dims, dtype=F32):
    return pltpu.VMEM(dims, dtype)


def left_body(grad_ref, error_ref, q_ref, p_ref, merged_ref, grad_buf, error_buf, q_buf, sems):
    plan, start = [], 0
    for at, size in enumerate(LEFT_CHUNKS):
        columns = pl.ds(start, size)
        copies = [
            pltpu.make_async_copy(ref.at[:, columns], buf.at[:, columns], sems.at[which, at])
            for which, (ref, buf) in enumerate(((grad_ref, grad_buf), (error_ref, error_buf), (q_ref, q_buf)))
        ]
        for copy in copies:
            copy.start()
        plan.append((slice(start, start + size), copies))
        start += size
    total = None
    for columns, copies in plan:
        for copy in copies:
            copy.wait()
        merged = grad_buf[:, columns].astype(F32) + error_buf[:, columns]
        merged_ref[:, columns] = merged
        left = jnp.concatenate(split3(q_buf[:, columns]), axis=0)
        right = jnp.concatenate(split3(merged), axis=0)
        product = dot(left, right, NT)
        total = product if total is None else total + product
    total = total[:RANK] + (total[RANK : 2 * RANK] + total[2 * RANK :])
    p_ref[...] = total[:, :ROWS] + (total[:, ROWS : 2 * ROWS] + total[:, 2 * ROWS :])


def left_product(grad, error, q_rows):
    return kernel_call(
        left_body,
        (in_vmem(RANK, ROWS), in_vmem(ROWS, WIDTH)),
        in_specs=[ANY] * 3,
        out_specs=(VMEM, VMEM),
        scratch_shapes=[
            pltpu.VMEM((ROWS, WIDTH), BF16),
            pltpu.VMEM((ROWS, WIDTH), F32),
            pltpu.VMEM((RANK, WIDTH), F32),
            pltpu.SemaphoreType.DMA((3, len(LEFT_CHUNKS))),
        ],
    )(*(pltpu.with_memory_space_constraint(value, pltpu.HBM) for value in (grad, error, q_rows)))


def one_row():
    return (lax.broadcasted_iota(jnp.int32, (8, LANES), 0) == lax.axis_index("dp") // 2).astype(F32)


def right_body(parts_ref, merged_ref, pieces_ref, p_ref):
    p_sum = jnp.sum(parts_ref[...], axis=0)
    p_ref[...] = p_sum
    p_parts = jnp.concatenate(split3(p_sum), axis=0)
    gram = lax.dot_general(p_sum, p_sum, NT, precision=HIGHEST, preferred_element_type=F32)
    packed = jnp.concatenate([gram[8 * a : 8 * a + 8] for a in range(4)], axis=1)
    row = 0.5 * jnp.sum(packed * one_row(), axis=0, keepdims=True)
    for half in range(2):
        h, m, l = split3(merged_ref[:, half * HALF : (half + 1) * HALF])
        with_h = dot(p_parts, h)
        with_m = dot(p_parts[: 2 * RANK], m)
        with_l = dot(p_parts[:RANK], l)
        small = with_h[2 * RANK :] + with_m[RANK:] + with_l
        product = with_h[:RANK] + (with_h[RANK : 2 * RANK] + with_m[:RANK] + small)
        for tile in range(TILES):
            pieces_ref[half, :, tile, :] = product[:, tile * LANES : (tile + 1) * LANES]
        pieces_ref[half, :, TILES, :] = jnp.broadcast_to(row, (RANK, LANES))
        pieces_ref[half, :, TILES + 1, :] = jnp.zeros((RANK, LANES), F32)


def right_product(parts, merged):
    return vmem_call(right_body, (in_vmem(2, RANK, PIECE, LANES), in_vmem(RANK, ROWS)))(parts, merged)


def plane_body(parts_ref, out_ref):
    rows = parts_ref[0]
    for member in range(1, PLANE):
        rows += parts_ref[member]
    apart = [sum(parts_ref[x * RING + a, TILES : TILES + 1, :] for x in range(NX)) for a in range(RING)]
    total = apart[FAR_FIRST[0]]
    for z in FAR_FIRST[1:]:
        total += apart[z]
    gram = jnp.where(lax.axis_index("dp") % 2 == 0, total * one_row(), jnp.concatenate(apart, axis=0))
    both = jnp.concatenate([rows, gram], axis=0)
    for member in range(RING):
        out_ref[member] = both


def line_body(parts_ref, out_ref):
    rows = parts_ref[0, :PIECE, :]
    for member in range(1, RING):
        rows += parts_ref[member, :PIECE, :]
    for member in range(PLANE):
        out_ref[member] = rows


def factor_body(replicas, parts_ref, p_ref, basis_ref, basis_stack_ref, inverse_stack_ref):
    packed = parts_ref[0, PIECE:, :]
    for member in range(1, RING):
        packed += parts_ref[member, PIECE:, :]
    gram = jnp.concatenate([packed[:, RANK * a : RANK * (a + 1)] for a in range(4)], axis=0)
    row = lax.broadcasted_iota(jnp.int32, (RANK, RANK), 0)
    column = lax.broadcasted_iota(jnp.int32, (RANK, RANK), 1)
    unit = jnp.where(row == column, 1.0, 0.0).astype(F32)
    work = jnp.concatenate([gram, unit], axis=1)
    below = lax.broadcasted_iota(jnp.int32, (RANK, 1), 0)
    inverse = []
    for j in range(RANK):
        pivot_row = work[j : j + 1, :]
        pivot = pivot_row[:, j : j + 1]
        inverse.append(pivot_row[:, RANK:] / jnp.sqrt(pivot))
        if j < RANK - 1:
            factor = jnp.where(below > j, work[:, j : j + 1] / pivot, 0.0)
            work = work - factor * pivot_row
    inverse = jnp.concatenate(inverse, axis=0)
    basis = lax.dot_general(inverse, p_ref[...], NN, precision=HIGHEST, preferred_element_type=F32)
    basis_ref[...] = basis
    basis_stack_ref[...] = stack_left(basis.T)
    inverse_stack_ref[...] = stack_left(inverse * (1.0 / replicas))


def final_body(parts_ref, inverse_ref, basis_ref, merged_ref, out_ref, q_ref, out_buf, q_buf, sems):
    copies = []
    for half in range(2):
        right = jnp.concatenate([parts_ref[half, :, tile, :] for tile in range(TILES)], axis=1)
        columns = slice(half * HALF, (half + 1) * HALF)
        q_new = dot(inverse_ref[...], stack_right(right))
        q_buf[:, columns] = q_new
        out_buf[:, columns] = merged_ref[:, columns] - dot(basis_ref[...], stack_right(q_new))
        for which, (buf, ref) in enumerate(((out_buf, out_ref), (q_buf, q_ref))):
            copies.append(pltpu.make_async_copy(buf.at[:, columns], ref.at[:, columns], sems.at[which, half]))
            copies[-1].start()
    for copy in copies:
        copy.wait()


def final(*operands):
    return kernel_call(
        final_body,
        (shape(ROWS, WIDTH), shape(RANK, WIDTH)),
        in_specs=[VMEM] * 4,
        out_specs=(ANY, ANY),
        scratch_shapes=[
            pltpu.VMEM((ROWS, WIDTH), F32),
            pltpu.VMEM((RANK, WIDTH), F32),
            pltpu.SemaphoreType.DMA((2, 2)),
        ],
    )(*(pltpu.with_memory_space_constraint(value, pltpu.VMEM) for value in operands))


def pick(values, at):
    return lax.dynamic_index_in_dim(values, at, keepdims=False)


def exchange(values, groups):
    return lax.all_to_all(values, AXES, 0, 0, axis_index_groups=groups)


def spread(value, groups):
    return exchange(jnp.broadcast_to(value[None], (len(groups[0]),) + value.shape), groups)


def both_cores(value):
    return lax.all_gather(value, AXES, axis_index_groups=CHIP_GROUPS)


def per_device(grad, error, q_prev):
    replicas = lax.axis_size("dp")
    dp = lax.axis_index("dp").astype(jnp.uint32)
    core = dp % 2
    p_local, merged = left_product(grad[0], error[0], q_prev.T)
    p_both, core, other = lax.optimization_barrier((both_cores(p_local), core, 1 - core))
    p_parts = spread(jnp.sum(p_both, axis=0), Y_GROUPS)

    pieces, p_sum = right_product(p_parts, merged)
    traded = both_cores(pick(pieces, other))
    pieces = exchange(pick(pieces, core) + pick(traded, other), PLANE_GROUPS)
    lines = vmem_call(plane_body, in_vmem(RING, PIECE + 8, LANES))(pieces)
    lines = exchange(lines, LINE_GROUPS)
    own = vmem_call(line_body, in_vmem(PLANE, PIECE, LANES))(lines)
    own = exchange(own, PLANE_GROUPS)
    basis, basis_stack, inverse_stack = vmem_call(
        functools.partial(factor_body, replicas),
        (shape(RANK, ROWS), in_vmem(ROWS, 6 * RANK, dtype=BF16), in_vmem(RANK, 6 * RANK, dtype=BF16)),
    )(lines, p_sum)
    whole = both_cores(own)
    new_error, q_new = final(whole, inverse_stack, basis_stack, merged)
    return (new_error[None], basis.T, q_new.T)


def solution(mesh):
    placed = (P("dp", "vocab", None), P("dp", "vocab", None), P())
    return jax.shard_map(
        per_device,
        mesh=mesh,
        in_specs=placed,
        out_specs=(P("dp", "vocab", None), P("vocab", None), P()),
        check_vma=False,
    )
```
